768 devices in a mesh: bx: 12 (over z), by: 64 (over x, y, core).
Axes of the slice: x: 4, y: 8, z: 12, core: 2. Of those that a mesh axis runs over, the one named last changes fastest.
Arguments:
- features: float32 [48, 256, 64, 128], P('bx', 'by'), may hold values from -6 to 6
- coords: float32 [48, 256, 3, 128], P('bx', 'by'), as said below
- centers: int32 [12, 64, 32, 128], P('bx', 'by'), may hold values from 0 to 2047, as said below
- neighbours: int32 [12, 64, 32, 128], P('bx', 'by'), may hold values from 0 to 4607, as said below
- live_blocks: int32 [12, 64], P('bx', 'by'), may hold values from 8 to 32, as said below
- w_center: bfloat16 [64, 64], replicated, may hold values from -0.75 to 0.75
- w_neigh: bfloat16 [64, 64], replicated, may hold values from -0.75 to 0.75
- w_radial: float32 [8, 64], replicated, may hold values from -3 to 3
- w_latent: bfloat16 [64, 64], replicated, may hold values from -1 to 1
- w_tensor: bfloat16 [64, 16], replicated, may hold values from -1 to 1
- w_mix: bfloat16 [64, 64], replicated, may hold values from -0.75 to 0.75
- w_env: bfloat16 [16, 64], replicated, may hold values from -3 to 3
- w_out: float32 [64], replicated, may hold values from -1.5 to 1.5
Outputs:
- energies: float32 [48, 256, 128], P('bx', 'by')
- forces: float32 [48, 256, 3, 128], P('bx', 'by')
The draws below stay inside these ranges and needn't reach their ends.
Inputs may be any that keep to these rules, and one draw needn't show every extreme that they name: `centers`: a center atom of the brick; all edges of one edge block have their center in the same cell; every live edge's center and neighbour lie in the same or adjacent cells and differ in slot by at most 8, never the same atom. `neighbours`: an atom of the extended brick in the center's cell or one of its eight neighbouring cells. `live_blocks`: each brick has either 32 // 4 or 32 live blocks; some brick has 32. `coords`: x and y offsets lie in 0 to 6, z in 0 to 40 and rises with the slot.
All inputs are finite; a program needn't handle non-finite values.
Results may differ from the reference program's by a relative error of at most 0.02.
Values sent between devices are 32-bit elements; how exact they have to be, the bound alone decides.
No kernel may reach another device: no remote copies, remote signals or barrier semaphores. Data moves between devices by JAX's collectives and lax.ppermute only.
A program may use at most 32 MiB of HBM per device.

```python
import jax
import jax.numpy as jnp
from jax import lax

LAT = 64
CH = 16
NB = 8
BLK = 128
CX = 4
CY = 4
SLOTS = 128
EB = 32
NCX = 48
NCY = 256
N_BX = 12
N_BY = 64


CELL_WIDTH = 6.0


SLAB_HEIGHT = 40.0


def edge_lists(key):
    shape = (N_BX, N_BY, EB, BLK)
    keys = jax.random.split(key, 5)
    cell = jnp.broadcast_to(jax.random.randint(keys[0], (N_BX, N_BY, EB, 1), 0, CX * CY), shape)
    slot = jax.random.randint(keys[1], shape, 0, SLOTS)
    step_x = jax.random.randint(keys[2], shape, -1, 2)
    step_y = jax.random.randint(keys[3], shape, -1, 2)
    reach = SLOTS // 16 + 1
    other = jnp.clip(slot + jax.random.randint(keys[4], shape, -reach + 1, reach), 0, SLOTS - 1)
    same = (step_x == 0) & (step_y == 0) & (other == slot)
    moved = jnp.where(slot == SLOTS - 1, slot - 1, slot + 1)
    other = jnp.where(same, moved, other)
    cell_x = cell // CY
    cell_y = cell % CY
    centers = (cell * SLOTS + slot).astype(jnp.int32)
    neighbours = (((cell_x + 1 + step_x) * (CY + 2) + cell_y + 1 + step_y) * SLOTS + other).astype(jnp.int32)
    return (centers, neighbours)


def draw_centers(key, part):
    return edge_lists(key)[0]


def draw_neighbours(key, part):
    return edge_lists(key)[1]


def draw_live_blocks(key, part):
    key = jax.random.fold_in(key, 5)
    keys = jax.random.split(key, 2)
    heavy = jax.random.randint(keys[0], (N_BX, N_BY), 0, 4) == 0
    counts = jnp.where(heavy, EB, EB // 4).reshape(-1)
    chosen = jax.random.randint(keys[1], (), 0, N_BX * N_BY)
    counts = counts.at[chosen].set(EB)
    return counts.reshape(N_BX, N_BY).astype(jnp.int32)


def draw_coords(key, part):
    key = jax.random.fold_in(key, 7)
    keys = jax.random.split(key, 3)
    shape = (CX * N_BX, CY * N_BY, SLOTS)
    flat_a = jax.random.uniform(keys[0], shape, jnp.float32)
    flat_b = jax.random.uniform(keys[1], shape, jnp.float32)
    rise = jax.random.uniform(keys[2], shape, jnp.float32)
    slots = jnp.arange(SLOTS).astype(jnp.float32)[None, None, :]
    height = (slots + rise) * (SLAB_HEIGHT / SLOTS)
    return jnp.stack([flat_a * CELL_WIDTH, flat_b * CELL_WIDTH, height], 2)


def steps_of(stream_key, shape, cuts, least, top_value):
    loudness = 1.0
    for dim, blocks in cuts:
        steps = jax.random.uniform(jax.random.fold_in(jax.random.fold_in(stream_key, 6), dim), (blocks,), jnp.float32, least / len(cuts), top_value / len(cuts))
        loudness = loudness * jnp.repeat(jnp.exp(steps), shape[dim] // blocks).reshape((-1,) + (1,) * (len(shape) - 1 - dim))
    return loudness


def gaussian(own_key, shape, deviation, limit, cuts=(), kind=jnp.bfloat16):
    drawn = deviation * jax.random.normal(own_key, shape, jnp.float32)
    if cuts:
        drawn = drawn * steps_of(own_key, shape, cuts, -0.22, 0.18)
    return jnp.clip(drawn, -limit, limit).astype(kind)


def setup_inputs(seed: int = 0) -> dict:
    seeds = jax.random.split(jax.random.key(seed), 14)
    features = gaussian(seeds[0], (NCX, NCY, LAT, SLOTS), 1.0, 6.0, ((0, 12), (1, 64)), jnp.float32)
    coords = draw_coords(jax.random.fold_in(seeds[13], 71), 0)
    centers = draw_centers(jax.random.fold_in(seeds[13], 71), 0)
    neighbours = draw_neighbours(jax.random.fold_in(seeds[13], 71), 0)
    live_blocks = draw_live_blocks(jax.random.fold_in(seeds[13], 71), 0)
    w_center = gaussian(seeds[5], (LAT, LAT), LAT ** -0.5, 0.75)
    w_neigh = gaussian(seeds[6], (LAT, LAT), LAT ** -0.5, 0.75)
    w_radial = gaussian(seeds[7], (NB, LAT), (NB // 2) ** -0.5, 3.0, (), jnp.float32)
    w_latent = gaussian(seeds[8], (LAT, LAT), (LAT // 2) ** -0.5, 1.0)
    w_tensor = gaussian(seeds[9], (LAT, CH), (LAT // 2) ** -0.5, 1.0)
    w_mix = gaussian(seeds[10], (LAT, LAT), LAT ** -0.5, 0.75)
    w_env = gaussian(seeds[11], (CH, LAT), (CH // 4) ** -0.5, 3.0)
    w_out = gaussian(seeds[12], (LAT,), (LAT // 4) ** -0.5, 1.5, (), jnp.float32)
    return dict(features=features, coords=coords, centers=centers, neighbours=neighbours, live_blocks=live_blocks, w_center=w_center, w_neigh=w_neigh, w_radial=w_radial, w_latent=w_latent, w_tensor=w_tensor, w_mix=w_mix, w_env=w_env, w_out=w_out)


CELL_WIDTH = 6.0
CUTOFF = 6.0
SOFTEN = 0.25

def edge_terms(delta, near_c, near_n, centers, live, w_radial, w_latent, w_tensor, w_mix, w_env, w_out, atoms):
    radius = jnp.sqrt(lax.optimization_barrier(jnp.sum(delta * delta, 0)) + SOFTEN)
    scaled = jnp.minimum(radius / CUTOFF, 1.0)
    envelope = (1.0 - scaled * scaled) ** 2
    orders = jnp.arange(1, w_radial.shape[0] + 1).astype(delta.dtype)
    basis = jnp.sin(orders[:, None] * jnp.pi * scaled[None, :])
    radial = jnp.dot(w_radial.T, basis, precision=lax.Precision.HIGHEST, preferred_element_type=jnp.float32)
    zeta = jax.nn.silu(near_c + near_n + radial).astype(jnp.bfloat16)
    latent = jax.nn.silu(jnp.dot(w_latent.T, zeta, preferred_element_type=jnp.float32)).astype(jnp.bfloat16)
    chan = jnp.dot(w_tensor.T, latent, preferred_element_type=jnp.float32)
    harm = jnp.concatenate([jnp.ones_like(radius)[None, :], delta / radius[None, :]], 0)
    weight = live * envelope
    spread = (chan[:, None, :] * harm[None, :, :]).reshape(-1, radius.shape[0]) * weight[None, :]
    gamma = jnp.zeros((spread.shape[0], atoms), spread.dtype).at[:, centers].add(spread)
    seen = gamma[:, centers].reshape(chan.shape[0], 4, -1)
    scal = lax.optimization_barrier(jnp.sum(seen * harm[None, :, :], 1)).astype(jnp.bfloat16)
    hidden = jnp.dot(w_mix.T, latent, preferred_element_type=jnp.float32) + jnp.dot(w_env.T, scal, preferred_element_type=jnp.float32)
    edge_energy = weight * lax.optimization_barrier(jnp.sum(w_out[:, None] * jax.nn.silu(hidden), 0))
    return (jnp.sum(edge_energy), edge_energy)

def brick(feat_ext, coord_ext, centers, neighbours, live_count, w_center, w_neigh, w_radial, w_latent, w_tensor, w_mix, w_env, w_out):
    wide_x, wide_y, slots = (feat_ext.shape[0], feat_ext.shape[1], feat_ext.shape[3])
    flat = jnp.moveaxis(feat_ext, 2, 0).reshape(feat_ext.shape[2], -1)
    table_c = jnp.dot(w_center.T.astype(flat.dtype), flat, precision=lax.Precision.HIGHEST, preferred_element_type=flat.dtype)
    table_n = jnp.dot(w_neigh.T.astype(flat.dtype), flat, precision=lax.Precision.HIGHEST, preferred_element_type=flat.dtype)
    anchor_x = jnp.arange(wide_x).astype(coord_ext.dtype) * CELL_WIDTH
    anchor_y = jnp.arange(wide_y).astype(coord_ext.dtype) * CELL_WIDTH
    place_x = coord_ext[:, :, 0, :] + anchor_x[:, None, None]
    place_y = coord_ext[:, :, 1, :] + anchor_y[None, :, None]
    place_z = coord_ext[:, :, 2, :]
    position = jnp.stack([place_x, place_y, place_z]).reshape(3, -1)
    inner_y = wide_y - 2
    cell = centers // slots
    center_ext = ((cell // inner_y + 1) * wide_y + cell % inner_y + 1) * slots + centers % slots
    blocks = jnp.arange(centers.shape[0], dtype=jnp.int32) // BLK
    live = (blocks < live_count).astype(coord_ext.dtype)
    delta = position[:, neighbours] - position[:, center_ext]
    near_c = table_c[:, center_ext]
    near_n = table_n[:, neighbours]
    atoms = (wide_x - 2) * inner_y * slots

    def energy_of(moved):
        return edge_terms(moved, near_c, near_n, centers, live, w_radial, w_latent, w_tensor, w_mix, w_env, w_out, atoms)
    total, pull, edge_energy = jax.vjp(energy_of, delta, has_aux=True)
    grad = pull(jnp.ones_like(total))[0]
    energies = jnp.zeros((atoms,), edge_energy.dtype).at[centers].add(edge_energy).reshape(wide_x - 2, inner_y, slots)
    push = jnp.zeros((3, wide_x * wide_y * slots), grad.dtype).at[:, center_ext].add(grad).at[:, neighbours].add(-grad)
    push = jnp.moveaxis(push.reshape(3, wide_x, wide_y, slots), 0, 2)
    return (energies, push)

def reference(features, coords, centers, neighbours, live_blocks, w_center, w_neigh, w_radial, w_latent, w_tensor, w_mix, w_env, w_out):
    wrapped_f = jnp.pad(features, ((1, 1), (1, 1), (0, 0), (0, 0)), mode='wrap')
    wrapped_c = jnp.pad(coords, ((1, 1), (1, 1), (0, 0), (0, 0)), mode='wrap')
    anchor = jnp.zeros((), jnp.int32)

    def one(device):
        row = (device // N_BY).astype(jnp.int32)
        column = (device % N_BY).astype(jnp.int32)
        start = (row * CX, column * CY, anchor, anchor)
        feat_ext = lax.dynamic_slice(wrapped_f, start, (CX + 2, CY + 2, LAT, SLOTS))
        coord_ext = lax.dynamic_slice(wrapped_c, start, (CX + 2, CY + 2, 3, SLOTS))
        return brick(feat_ext, coord_ext, centers[row, column].reshape(-1), neighbours[row, column].reshape(-1), live_blocks[row, column], w_center, w_neigh, w_radial, w_latent, w_tensor, w_mix, w_env, w_out)
    energy_all, push_all = lax.map(one, jnp.arange(N_BX * N_BY, dtype=jnp.int32))
    energies = energy_all.reshape(N_BX, N_BY, CX, CY, SLOTS).transpose(0, 2, 1, 3, 4).reshape(CX * N_BX, CY * N_BY, SLOTS)
    padded = jnp.zeros((CX * N_BX + 2, CY * N_BY + 2, 3, SLOTS), push_all.dtype)

    def place(device, acc):
        row = (device // N_BY).astype(jnp.int32)
        column = (device % N_BY).astype(jnp.int32)
        start = (row * CX, column * CY, anchor, anchor)
        piece = push_all[device]
        current = lax.dynamic_slice(acc, start, piece.shape)
        return lax.dynamic_update_slice(acc, current + piece, start)
    padded = lax.fori_loop(0, N_BX * N_BY, place, padded)
    padded = padded.at[1].add(padded[-1]).at[-2].add(padded[0])[1:-1]
    padded = padded.at[:, 1].add(padded[:, -1]).at[:, -2].add(padded[:, 0])[:, 1:-1]
    return (energies, padded)
```

```python
import jax
import jax.numpy as jnp
from jax import lax
from jax.experimental import pallas as pl
from jax.experimental.pallas import tpu as pltpu
from jax.sharding import PartitionSpec as P

CELL_WIDTH = 6.0
CUTOFF = 6.0
SOFTEN = 0.25
ROWS = 72
GROUP = 8
F32 = jnp.float32
BF16 = jnp.bfloat16
SIN_TERMS = (3.14159265358979, -5.16771278004997, 2.55016403987735, -0.599264529320792, 0.0821458866111282, -0.00737043094571435)
COS_TERMS = (1.0, -4.93480220054468, 4.05871212641677, -1.33526276885459, 0.235330630358893, -0.0258068913900141, 0.00192957430940392)


def shifted(array, axis, by):
    length = lax.axis_size(axis)
    return lax.ppermute(array, axis, [(i, (i + by) % length) for i in range(length)])


def split(array):
    high = array.astype(BF16).astype(F32)
    return high, array - high


def dot_tn(left, right):
    return lax.dot_general(left, right, (((0,), (0,)), ((), ())), preferred_element_type=F32)


def dot_nt(left, right):
    return lax.dot_general(left, right, (((1,), (1,)), ((), ())), preferred_element_type=F32)


def dot_nn(left, right):
    return jnp.dot(left, right, preferred_element_type=F32)


def tables_kernel(feat, coord, w_center, w_neigh, table_c, packed):
    inner_x, inner_y, lat, slots = feat.shape
    both = jnp.concatenate([w_center[...].astype(F32), w_neigh[...].astype(F32)], 1)
    both = jnp.concatenate([both, both], 0).T.astype(BF16)
    pad = jnp.zeros((ROWS - lat - 3, slots), F32)
    for x in range(inner_x):
        flat = jnp.concatenate([feat[x, y] for y in range(inner_y)], 1)
        high, low = split(flat)
        out = dot_nn(both, jnp.concatenate([high, low], 0).astype(BF16))
        for y in range(inner_y):
            piece = out[:, y * slots : (y + 1) * slots]
            table_c[x * inner_y + y] = piece[:lat]
            packed[x, y, :lat] = piece[lat:]
            packed[x, y, lat:] = jnp.concatenate([coord[x, y], pad], 0)


def tables(features, coords, w_center, w_neigh):
    inner_x, inner_y, lat, slots = features.shape
    return pl.pallas_call(
        tables_kernel,
        out_shape=(
            jax.ShapeDtypeStruct((inner_x * inner_y, lat, slots), F32),
            jax.ShapeDtypeStruct((inner_x, inner_y, ROWS, slots), F32),
        ),
        compiler_params=pltpu.CompilerParams(vmem_limit_bytes=16 * 1024 * 1024),
    )(features, coords, w_center, w_neigh)


def sine_cosine(turns):
    whole = jnp.floor(turns + 0.5)
    part = turns - whole
    sign = 1.0 - 2.0 * (whole - 2.0 * jnp.floor(0.5 * whole))
    square = part * part

    def poly(terms):
        total = jnp.full_like(square, terms[-1])
        for term in terms[-2::-1]:
            total = total * square + term
        return total

    return sign * part * poly(SIN_TERMS), sign * poly(COS_TERMS)


def gated(value):
    gate = 0.5 * jnp.tanh(0.5 * value) + 0.5
    silu = value * gate
    return silu, gate + silu - silu * gate


def brick_kernel(
    cells,
    live,
    centers,
    neighbours,
    table_c,
    packed,
    west,
    east,
    south,
    north,
    w_radial,
    w_latent,
    w_tensor,
    w_mix,
    w_env,
    w_out,
    energies,
    push_west,
    push_east,
    push_inner,
    table_n,
    gamma,
    g_gamma,
    push,
    slope_z,
    slope_l,
    latent_s,
    g_hidden_s,
    chan_s,
    rows_s,
    sems,
):
    inner_x, inner_y, _, slots = packed.shape
    wide_y = inner_y + 2
    lat = w_latent.shape[0]
    ch = w_tensor.shape[1]
    nb = w_radial.shape[0]
    width = GROUP * slots
    copies = []
    for x in range(inner_x):
        copies.append((packed.at[x], (x + 1) * wide_y + 1, inner_y))
    copies.append((west.at[0], 1, inner_y))
    copies.append((east.at[0], (inner_x + 1) * wide_y + 1, inner_y))
    for x in range(inner_x + 2):
        copies.append((south.at[x], x * wide_y, 1))
        copies.append((north.at[x], x * wide_y + inner_y + 1, 1))
    started = []
    for i, (source, at, count) in enumerate(copies):
        copy = pltpu.make_async_copy(source, table_n.at[pl.ds(at, count)], sems.at[i])
        copy.start()
        started.append(copy)

    gamma[...] = jnp.zeros_like(gamma)
    g_gamma[...] = jnp.zeros_like(g_gamma)
    push[...] = jnp.zeros_like(push)
    wr_high, wr_low = split(w_radial[...])
    wr_fwd = jnp.concatenate([wr_high, wr_high, wr_low, wr_low], 0).astype(BF16)
    wr_bwd = jnp.concatenate([wr_high, wr_low], 0).astype(BF16)
    orders = lax.broadcasted_iota(jnp.int32, (nb, 1), 0).astype(F32) + 1.0
    slot_iota = lax.broadcasted_iota(jnp.int32, (slots, slots), 0)
    row_iota = lax.broadcasted_iota(jnp.int32, (8, 1), 0)
    force_rows = jnp.where((row_iota & 3) == 3, 0.0, 1.0)
    out_col = w_out[...]
    offsets = [dx * wide_y + dy for dx in (-1, 0, 1) for dy in (-1, 0, 1)]
    groups = live[0, 0] // GROUP
    for copy in started:
        copy.wait()

    def cell_of(block):
        cell = cells[0, 0, block, 0] // slots
        cell_x = cell // inner_y
        return cell, (cell_x + 1) * wide_y + (cell - cell_x * inner_y) + 1

    def hot(slot):
        return jnp.where(slot_iota == slot, 1.0, 0.0).astype(BF16)

    def lanes(array, j):
        return array[:, j * slots : (j + 1) * slots]

    def gathered(table, slot_rows, blocks):
        parts = []
        for j in range(GROUP):
            cell, _ = cell_of(blocks + j)
            index = jnp.broadcast_to(slot_rows[j : j + 1], (4 * ch, slots))
            parts.append(jnp.take_along_axis(table[cell], index, axis=1))
        return jnp.concatenate(parts, 1)

    def scattered(table, values, slot_rows, blocks):
        for j in range(GROUP):
            cell, _ = cell_of(blocks + j)
            out = dot_nt(lanes(values, j).astype(BF16), hot(slot_rows[j : j + 1]))
            rows = table.shape[1]
            table[cell] += sum(out[i : i + rows] for i in range(0, out.shape[0], rows))

    def forward(g, carry):
        blocks = pl.multiple_of(g * GROUP, GROUP)
        c_rows = centers[0, 0, pl.ds(blocks, GROUP), :] & (slots - 1)
        n_all = neighbours[0, 0, pl.ds(blocks, GROUP), :]
        n_rows = n_all & (slots - 1)
        n_cells = n_all >> 7
        n_x = (n_cells * 43) >> 8
        n_y = n_cells - n_x * wide_y
        near_parts, delta_parts = [], []
        for j in range(GROUP):
            cell, ext = cell_of(blocks + j)
            ext_x = cell // inner_y + 1
            ext_y = cell - (ext_x - 1) * inner_y + 1
            c_index = jnp.broadcast_to(c_rows[j : j + 1], (lat, slots))
            n_index = jnp.broadcast_to(n_rows[j : j + 1], (ROWS, slots))
            n_cell = jnp.broadcast_to(n_cells[j : j + 1] - ext, (ROWS, slots))
            near_c = jnp.take_along_axis(table_c[cell], c_index, axis=1)
            place_c = jnp.take_along_axis(table_n[ext, lat:], c_index[:8], axis=1)
            got = jnp.zeros((ROWS, slots), F32)
            for offset in offsets:
                piece = jnp.take_along_axis(table_n[ext + offset], n_index, axis=1)
                got = jnp.where(n_cell == offset, piece, got)
            near_parts.append(near_c + got[:lat])
            step_x = (n_x[j : j + 1] - ext_x).astype(F32) * CELL_WIDTH
            step_y = (n_y[j : j + 1] - ext_y).astype(F32) * CELL_WIDTH
            step = jnp.where(row_iota == 0, step_x, jnp.where(row_iota == 1, step_y, 0.0))
            delta_parts.append(got[lat:] - place_c + step)
        near = jnp.concatenate(near_parts, 1)
        delta = jnp.concatenate(delta_parts, 1)
        square = delta * delta
        length2 = square[0:1] + square[1:2] + square[2:3] + SOFTEN
        inverse = lax.rsqrt(length2)
        scaled = jnp.minimum(length2 * inverse * (1.0 / CUTOFF), 1.0)
        fall = 1.0 - scaled * scaled
        weight = fall * fall
        harm = delta * inverse
        basis, _ = sine_cosine(orders * scaled)
        b_high, b_low = split(basis)
        b_all = jnp.concatenate([b_high, b_low, b_high, b_low], 0).astype(BF16)
        zeta, slope = gated(near + dot_tn(wr_fwd, b_all))
        slope_z[g] = slope
        latent, slope = gated(dot_tn(w_latent[...], zeta.astype(BF16)))
        slope_l[g] = slope
        latent = latent.astype(BF16)
        latent_s[g] = latent
        chan = dot_tn(w_tensor[...], latent)
        chan_s[g] = chan
        rows_s[g, 0:3] = harm[0:3]
        rows_s[g, 3:4] = weight
        rows_s[g, 4:5] = scaled
        rows_s[g, 5:6] = inverse
        heavy = chan * weight
        spread = jnp.concatenate([heavy] + [heavy * harm[m : m + 1] for m in range(3)], 0)
        scattered(gamma, jnp.concatenate(split(spread), 0), c_rows, blocks)
        return carry

    lax.fori_loop(0, groups, forward, 0)

    def middle(g, carry):
        blocks = pl.multiple_of(g * GROUP, GROUP)
        c_rows = centers[0, 0, pl.ds(blocks, GROUP), :] & (slots - 1)
        seen = gathered(gamma, c_rows, blocks)
        weight = rows_s[g, 3:4]
        harm = [rows_s[g, m : m + 1] for m in range(3)]
        scal = seen[:ch]
        for m in range(3):
            scal = scal + harm[m] * seen[(m + 1) * ch : (m + 2) * ch]
        hidden = dot_tn(w_mix[...], latent_s[g]) + dot_tn(w_env[...], scal.astype(BF16))
        lifted, slope = gated(hidden)
        value = jnp.sum(out_col * lifted, 0, keepdims=True)
        g_hidden = ((out_col * slope) * weight).astype(BF16)
        g_hidden_s[g] = g_hidden
        g_scal = dot_nn(w_env[...], g_hidden)
        rows_s[g, 6:7] = value
        for m in range(3):
            rows_s[g, 8 + m : 9 + m] = jnp.sum(g_scal * seen[(m + 1) * ch : (m + 2) * ch], 0, keepdims=True)
        spread = jnp.concatenate([g_scal] + [g_scal * harm[m] for m in range(3)], 0)
        scattered(g_gamma, spread, c_rows, blocks)
        return carry

    lax.fori_loop(0, groups, middle, 0)

    def backward(g, carry):
        blocks = pl.multiple_of(g * GROUP, GROUP)
        c_rows = centers[0, 0, pl.ds(blocks, GROUP), :] & (slots - 1)
        n_all = neighbours[0, 0, pl.ds(blocks, GROUP), :]
        n_rows = n_all & (slots - 1)
        n_cells = n_all >> 7
        back = gathered(g_gamma, c_rows, blocks)
        harm = [rows_s[g, m : m + 1] for m in range(3)]
        weight = rows_s[g, 3:4]
        scaled = rows_s[g, 4:5]
        inverse = rows_s[g, 5:6]
        value = rows_s[g, 6:7]
        chan = chan_s[g]
        g_weight = value
        g_chan = jnp.zeros_like(chan)
        g_harm = []
        for m in range(4):
            part = back[m * ch : (m + 1) * ch]
            along = jnp.sum(chan * part, 0, keepdims=True)
            if m == 0:
                g_weight = g_weight + along
                g_chan = g_chan + part
            else:
                g_weight = g_weight + along * harm[m - 1]
                g_chan = g_chan + part * harm[m - 1]
                g_harm.append(rows_s[g, 7 + m : 8 + m] + weight * along)
        g_chan = (g_chan * weight).astype(BF16)
        g_latent = dot_nn(w_mix[...], g_hidden_s[g]) + dot_nn(w_tensor[...], g_chan)
        g_zeta = dot_nn(w_latent[...], (g_latent * slope_l[g]).astype(BF16))
        g_pair = dot_nn(wr_bwd, (g_zeta * slope_z[g]).astype(BF16))
        _, cosines = sine_cosine(orders * scaled)
        turning = (3.14159265358979 * orders) * cosines
        g_scaled = jnp.sum((g_pair[:nb] + g_pair[nb:]) * turning, 0, keepdims=True)
        g_scaled = jnp.where(scaled < 1.0, g_scaled, 0.0)
        g_scaled = g_scaled - 4.0 * scaled * (1.0 - scaled * scaled) * g_weight
        radial = g_harm[0] * harm[0] + g_harm[1] * harm[1] + g_harm[2] * harm[2]
        pull = g_scaled * (1.0 / CUTOFF) - radial * inverse
        grads = [g_harm[m] * inverse + harm[m] * pull for m in range(3)]
        four = jnp.concatenate(grads + [weight * value], 0)
        high, low = split(four)
        eight = jnp.concatenate([high, low], 0)
        eight_n = eight * force_rows
        for j in range(GROUP):
            _, ext = cell_of(blocks + j)
            push[ext] += dot_nt(lanes(eight, j).astype(BF16), hot(c_rows[j : j + 1]))
            mine = lanes(eight_n, j)
            n_cell = n_cells[j : j + 1] - ext
            spread = jnp.concatenate([jnp.where(n_cell == offset, mine, 0.0) for offset in offsets], 0)
            out = dot_nt(spread.astype(BF16), hot(n_rows[j : j + 1]))
            for i, offset in enumerate(offsets):
                push[ext + offset] -= out[8 * i : 8 * i + 8]
        return carry

    lax.fori_loop(0, groups, backward, 0)

    for x in range(inner_x + 2):
        for y in range(wide_y):
            both = push[x * wide_y + y]
            total = both[0:4] + both[4:8]
            if x == 0:
                push_west[y] = total[:3]
            elif x == inner_x + 1:
                push_east[y] = total[:3]
            else:
                push_inner[x - 1, y] = total[:3]
                if 1 <= y <= inner_y:
                    energies[x - 1, y - 1 : y] = total[3:4]


def brick(centers, neighbours, live_blocks, table_c, packed, west, east, south, north, *weights):
    inner_x, inner_y, rows, slots = packed.shape
    blocks = centers.shape[2]
    lat = table_c.shape[1]
    ch = weights[2].shape[1]
    wide_y = inner_y + 2
    cells_ext = (inner_x + 2) * wide_y
    groups = blocks // GROUP
    width = GROUP * slots
    vmem = pl.BlockSpec(memory_space=pltpu.VMEM)
    smem = pl.BlockSpec(memory_space=pltpu.SMEM)
    anywhere = pl.BlockSpec(memory_space=pl.ANY)
    return pl.pallas_call(
        brick_kernel,
        in_specs=[smem, smem, vmem, vmem, vmem] + [anywhere] * 5 + [vmem] * 6,
        out_specs=(vmem,) * 4,
        out_shape=(
            jax.ShapeDtypeStruct((inner_x, inner_y, slots), F32),
            jax.ShapeDtypeStruct((wide_y, 3, slots), F32),
            jax.ShapeDtypeStruct((wide_y, 3, slots), F32),
            jax.ShapeDtypeStruct((inner_x, wide_y, 3, slots), F32),
        ),
        scratch_shapes=[
            pltpu.VMEM((cells_ext, rows, slots), F32),
            pltpu.VMEM((inner_x * inner_y, 4 * ch, slots), F32),
            pltpu.VMEM((inner_x * inner_y, 4 * ch, slots), F32),
            pltpu.VMEM((cells_ext, 8, slots), F32),
            pltpu.VMEM((groups, lat, width), F32),
            pltpu.VMEM((groups, lat, width), F32),
            pltpu.VMEM((groups, lat, width), BF16),
            pltpu.VMEM((groups, lat, width), BF16),
            pltpu.VMEM((groups, ch, width), F32),
            pltpu.VMEM((groups, 16, width), F32),
            pltpu.SemaphoreType.DMA((inner_x + 2 + 2 * (inner_x + 2),)),
        ],
        compiler_params=pltpu.CompilerParams(vmem_limit_bytes=40 * 1024 * 1024),
    )(centers, live_blocks, centers, neighbours, table_c, packed, west, east, south, north, *weights)


def body(
    features,
    coords,
    centers,
    neighbours,
    live_blocks,
    w_center,
    w_neigh,
    w_radial,
    w_latent,
    w_tensor,
    w_mix,
    w_env,
    w_out,
):
    table_c, packed = tables(features, coords, w_center, w_neigh)
    inner_x, inner_y = packed.shape[:2]
    west = shifted(packed[inner_x - 1 :], "bx", 1)
    east = shifted(packed[:1], "bx", -1)
    top = jnp.concatenate([west[:, inner_y - 1], packed[:, inner_y - 1], east[:, inner_y - 1]], 0)
    bottom = jnp.concatenate([west[:, 0], packed[:, 0], east[:, 0]], 0)
    south = shifted(top[:, None], "by", 1)
    north = shifted(bottom[:, None], "by", -1)
    weights = (w_radial, w_latent, w_tensor, w_mix, w_env, w_out[:, None])
    energies, push_west, push_east, inner = brick(
        centers, neighbours, live_blocks, table_c, packed, west, east, south, north, *weights
    )
    from_east = shifted(push_west, "bx", -1)
    from_west = shifted(push_east, "bx", 1)
    inner = inner.at[inner_x - 1].add(from_east).at[0].add(from_west)
    from_north = shifted(inner[:, 0], "by", -1)
    from_south = shifted(inner[:, inner_y + 1], "by", 1)
    forces = inner[:, 1 : inner_y + 1]
    forces = forces.at[:, inner_y - 1].add(from_north).at[:, 0].add(from_south)
    return (energies, forces)


def solution(mesh):
    split_both = P("bx", "by", None, None)
    placed = (split_both,) * 4 + (P("bx", "by"),) + (P(),) * 8
    return jax.shard_map(
        body,
        mesh=mesh,
        in_specs=placed,
        out_specs=(P("bx", "by", None), split_both),
        check_vma=False,
    )
```

```python
import jax
import jax.numpy as jnp
from jax import lax
from jax.experimental import pallas as pl
from jax.experimental.pallas import tpu as pltpu
from jax.sharding import PartitionSpec as P

CELL_WIDTH = 6.0
CUTOFF = 6.0
SOFTEN = 0.25
ROWS = 72
GROUP = 32
F32 = jnp.float32
BF16 = jnp.bfloat16
SIN_TERMS = (3.14159265358979, -5.16771278004997, 2.55016403987735, -0.599264529320792, 0.0821458866111282, -0.00737043094571435)
COS_TERMS = (1.0, -4.93480220054468, 4.05871212641677, -1.33526276885459, 0.235330630358893, -0.0258068913900141, 0.00192957430940392)


def shifted(array, axis, by):
    length = lax.axis_size(axis)
    return lax.ppermute(array, axis, [(i, (i + by) % length) for i in range(length)])


def split(array):
    high = array.astype(BF16).astype(F32)
    return high, array - high


def dot_tn(left, right):
    return lax.dot_general(left, right, (((0,), (0,)), ((), ())), preferred_element_type=F32)


def dot_nt(left, right):
    return lax.dot_general(left, right, (((1,), (1,)), ((), ())), preferred_element_type=F32)


def dot_nn(left, right):
    return jnp.dot(left, right, preferred_element_type=F32)


def tables_kernel(feat, coord, w_center, w_neigh, table_c, packed):
    inner_x, inner_y, lat, slots = feat.shape
    both = 0.5 * jnp.concatenate([w_center[...].astype(F32), w_neigh[...].astype(F32)], 1)
    both = jnp.concatenate([both, both], 0).T.astype(BF16)
    pad = jnp.zeros((ROWS - lat - 3, slots), F32)
    for x in range(inner_x):
        flat = jnp.concatenate([feat[x, y] for y in range(inner_y)], 1)
        high, low = split(flat)
        out = dot_nn(both, jnp.concatenate([high, low], 0).astype(BF16))
        for y in range(inner_y):
            piece = out[:, y * slots : (y + 1) * slots]
            table_c[x * inner_y + y] = piece[:lat]
            packed[x, y, :lat] = piece[lat:]
            packed[x, y, lat:] = jnp.concatenate([coord[x, m, y : y + 1] for m in range(3)] + [pad], 0)


def tables(features, coords, w_center, w_neigh):
    inner_x, inner_y, lat, slots = features.shape
    return pl.pallas_call(
        tables_kernel,
        out_shape=(
            jax.ShapeDtypeStruct((inner_x * inner_y, lat, slots), F32),
            jax.ShapeDtypeStruct((inner_x, inner_y, ROWS, slots), F32),
        ),
        compiler_params=pltpu.CompilerParams(vmem_limit_bytes=16 * 1024 * 1024),
    )(features, coords, w_center, w_neigh)


def sine_cosine(turns):
    whole = jnp.floor(turns + 0.5)
    part = turns - whole
    sign = 1.0 - 2.0 * (whole - 2.0 * jnp.floor(0.5 * whole))
    square = part * part

    def poly(terms):
        total = jnp.full_like(square, terms[-1])
        for term in terms[-2::-1]:
            total = total * square + term
        return total

    return sign * part * poly(SIN_TERMS), sign * poly(COS_TERMS)


def gated(half):
    gate = 1.0 + jnp.tanh(half)
    silu = half * gate
    return silu, gate + silu * (2.0 - gate)


def halved(array):
    return (array.astype(F32) * 0.5).astype(array.dtype)


def brick_kernel(
    cells,
    live,
    centers,
    neighbours,
    table_c,
    packed,
    west,
    east,
    south,
    north,
    w_radial,
    w_latent,
    w_tensor,
    w_mix,
    w_env,
    w_out,
    energies,
    push_west,
    push_east,
    push_inner,
    table_n,
    gamma,
    g_gamma,
    push,
    slope_z,
    slope_l,
    latent_s,
    g_hidden_s,
    chan_s,
    rows_s,
):
    inner_x, inner_y, _, slots = packed.shape
    wide_y = inner_y + 2
    lat = w_latent.shape[0]
    ch = w_tensor.shape[1]
    nb = w_radial.shape[0]
    width = GROUP * slots
    for x in range(inner_x + 2):
        for y in range(wide_y):
            if y == 0:
                source = south[x, 0]
            elif y == inner_y + 1:
                source = north[x, 0]
            elif x == 0:
                source = west[0, y - 1]
            elif x == inner_x + 1:
                source = east[0, y - 1]
            else:
                source = packed[x - 1, y - 1]
            table_n[x * wide_y + y] = source
    gamma[...] = jnp.zeros_like(gamma)
    g_gamma[...] = jnp.zeros_like(g_gamma)
    push[...] = jnp.zeros_like(push)
    wr_high, wr_low = split(0.5 * w_radial[...])
    half_latent, half_mix, half_env = halved(w_latent[...]), halved(w_mix[...]), halved(w_env[...])
    wr_fwd = jnp.concatenate([wr_high, wr_high, wr_low, wr_low], 0).astype(BF16)
    wr_bwd = jnp.concatenate([wr_high, wr_low], 0).astype(BF16)
    orders = lax.broadcasted_iota(jnp.int32, (nb, 1), 0).astype(F32) + 1.0
    slot_iota = lax.broadcasted_iota(jnp.int32, (slots, slots), 0)
    row_iota = lax.broadcasted_iota(jnp.int32, (8, 1), 0)
    force_rows = jnp.where((row_iota & 3) == 3, 0.0, 1.0)
    out_col = w_out[...]
    half_col = 0.5 * out_col
    offsets = [dx * wide_y + dy for dx in (-1, 0, 1) for dy in (-1, 0, 1)]
    groups = (live[0, 0] + (GROUP - 1)) // GROUP
    block_iota = lax.broadcasted_iota(jnp.int32, (1, width), 1) // slots

    def cell_of(block):
        cell = cells[0, block] // slots
        cell_x = cell // inner_y
        return cell, (cell_x + 1) * wide_y + (cell - cell_x * inner_y) + 1

    def hot(slot):
        return jnp.where(slot_iota == slot, 1.0, 0.0).astype(BF16)

    def lanes(array, j):
        return array[:, j * slots : (j + 1) * slots]

    def gathered(table, slot_rows, blocks):
        parts = []
        for j in range(GROUP):
            cell, _ = cell_of(blocks + j)
            index = jnp.broadcast_to(slot_rows[j : j + 1], (4 * ch, slots))
            parts.append(jnp.take_along_axis(table[cell], index, axis=1))
        return jnp.concatenate(parts, 1)

    def scattered(table, values, slot_rows, blocks):
        for j in range(GROUP):
            cell, _ = cell_of(blocks + j)
            out = dot_nt(lanes(values, j).astype(BF16), hot(slot_rows[j : j + 1]))
            rows = table.shape[1]
            table[cell] += sum(out[i : i + rows] for i in range(0, out.shape[0], rows))

    def forward(g, carry):
        blocks = pl.multiple_of(g * GROUP, GROUP)
        c_rows = centers[0, 0, pl.ds(blocks, GROUP), :] & (slots - 1)
        n_all = neighbours[0, 0, pl.ds(blocks, GROUP), :]
        n_rows = n_all & (slots - 1)
        n_cells = n_all >> 7
        n_x = (n_cells * 43) >> 8
        n_y = n_cells - n_x * wide_y
        near_parts, delta_parts = [], []
        for j in range(GROUP):
            cell, ext = cell_of(blocks + j)
            ext_x = cell // inner_y + 1
            ext_y = cell - (ext_x - 1) * inner_y + 1
            c_index = jnp.broadcast_to(c_rows[j : j + 1], (lat, slots))
            n_index = jnp.broadcast_to(n_rows[j : j + 1], (ROWS, slots))
            n_cell = jnp.broadcast_to(n_cells[j : j + 1] - ext, (ROWS, slots))
            near_c = jnp.take_along_axis(table_c[cell], c_index, axis=1)
            place_c = jnp.take_along_axis(table_n[ext, lat:], c_index[:8], axis=1)
            got = jnp.zeros((ROWS, slots), F32)
            for offset in offsets:
                piece = jnp.take_along_axis(table_n[ext + offset], n_index, axis=1)
                got = jnp.where(n_cell == offset, piece, got)
            near_parts.append(near_c + got[:lat])
            step_x = (n_x[j : j + 1] - ext_x).astype(F32) * CELL_WIDTH
            step_y = (n_y[j : j + 1] - ext_y).astype(F32) * CELL_WIDTH
            step = jnp.where(row_iota == 0, step_x, jnp.where(row_iota == 1, step_y, 0.0))
            delta_parts.append(got[lat:] - place_c + step)
        near = jnp.concatenate(near_parts, 1)
        delta = jnp.concatenate(delta_parts, 1)
        square = delta * delta
        length2 = square[0:1] + square[1:2] + square[2:3] + SOFTEN
        inverse = lax.rsqrt(length2)
        scaled = jnp.minimum(length2 * inverse * (1.0 / CUTOFF), 1.0)
        fall = 1.0 - scaled * scaled
        weight = jnp.where(block_iota + blocks < live[0, 0], fall * fall, 0.0)
        harm = delta * inverse
        basis, _ = sine_cosine(orders * scaled)
        b_high, b_low = split(basis)
        b_all = jnp.concatenate([b_high, b_low, b_high, b_low], 0).astype(BF16)
        zeta, slope = gated(near + dot_tn(wr_fwd, b_all))
        slope_z[g] = slope
        latent, slope = gated(dot_tn(half_latent, zeta.astype(BF16)))
        slope_l[g] = slope
        latent = latent.astype(BF16)
        latent_s[g] = latent
        chan = dot_tn(w_tensor[...], latent)
        chan_s[g] = chan
        rows_s[g, 0:3] = harm[0:3]
        rows_s[g, 3:4] = weight
        rows_s[g, 4:5] = scaled
        rows_s[g, 5:6] = inverse
        heavy = chan * weight
        spread = jnp.concatenate([heavy] + [heavy * harm[m : m + 1] for m in range(3)], 0)
        scattered(gamma, jnp.concatenate(split(spread), 0), c_rows, blocks)
        return carry

    lax.fori_loop(0, groups, forward, 0)

    def middle(g, carry):
        blocks = pl.multiple_of(g * GROUP, GROUP)
        c_rows = centers[0, 0, pl.ds(blocks, GROUP), :] & (slots - 1)
        seen = gathered(gamma, c_rows, blocks)
        weight = rows_s[g, 3:4]
        harm = [rows_s[g, m : m + 1] for m in range(3)]
        scal = seen[:ch]
        for m in range(3):
            scal = scal + harm[m] * seen[(m + 1) * ch : (m + 2) * ch]
        hidden = dot_tn(half_mix, latent_s[g]) + dot_tn(half_env, scal.astype(BF16))
        lifted, slope = gated(hidden)
        value = jnp.sum(out_col * lifted, 0, keepdims=True)
        g_hidden = ((half_col * slope) * weight).astype(BF16)
        g_hidden_s[g] = g_hidden
        g_scal = dot_nn(w_env[...], g_hidden)
        rows_s[g, 6:7] = value
        for m in range(3):
            rows_s[g, 8 + m : 9 + m] = jnp.sum(g_scal * seen[(m + 1) * ch : (m + 2) * ch], 0, keepdims=True)
        spread = jnp.concatenate([g_scal] + [g_scal * harm[m] for m in range(3)], 0)
        scattered(g_gamma, spread, c_rows, blocks)
        return carry

    lax.fori_loop(0, groups, middle, 0)

    def backward(g, carry):
        blocks = pl.multiple_of(g * GROUP, GROUP)
        c_rows = centers[0, 0, pl.ds(blocks, GROUP), :] & (slots - 1)
        n_all = neighbours[0, 0, pl.ds(blocks, GROUP), :]
        n_rows = n_all & (slots - 1)
        n_cells = n_all >> 7
        back = gathered(g_gamma, c_rows, blocks)
        harm = [rows_s[g, m : m + 1] for m in range(3)]
        weight = rows_s[g, 3:4]
        scaled = rows_s[g, 4:5]
        inverse = rows_s[g, 5:6]
        value = rows_s[g, 6:7]
        chan = chan_s[g]
        g_weight = value
        g_chan = jnp.zeros_like(chan)
        g_harm = []
        for m in range(4):
            part = back[m * ch : (m + 1) * ch]
            along = jnp.sum(chan * part, 0, keepdims=True)
            if m == 0:
                g_weight = g_weight + along
                g_chan = g_chan + part
            else:
                g_weight = g_weight + along * harm[m - 1]
                g_chan = g_chan + part * harm[m - 1]
                g_harm.append(rows_s[g, 7 + m : 8 + m] + weight * along)
        g_chan = (g_chan * weight).astype(BF16)
        g_latent = dot_nn(w_mix[...], g_hidden_s[g]) + dot_nn(w_tensor[...], g_chan)
        g_zeta = dot_nn(half_latent, (g_latent * slope_l[g]).astype(BF16))
        g_pair = dot_nn(wr_bwd, (g_zeta * slope_z[g]).astype(BF16))
        _, cosines = sine_cosine(orders * scaled)
        turning = (3.14159265358979 * orders) * cosines
        g_scaled = jnp.sum((g_pair[:nb] + g_pair[nb:]) * turning, 0, keepdims=True)
        g_scaled = jnp.where(scaled < 1.0, g_scaled, 0.0)
        g_weight = jnp.where(block_iota + blocks < live[0, 0], g_weight, 0.0)
        g_scaled = g_scaled - 4.0 * scaled * (1.0 - scaled * scaled) * g_weight
        radial = g_harm[0] * harm[0] + g_harm[1] * harm[1] + g_harm[2] * harm[2]
        pull = g_scaled * (1.0 / CUTOFF) - radial * inverse
        grads = [g_harm[m] * inverse + harm[m] * pull for m in range(3)]
        four = jnp.concatenate(grads + [weight * value], 0)
        high, low = split(four)
        eight = jnp.concatenate([high, low], 0)
        eight_n = eight * force_rows
        for j in range(GROUP):
            _, ext = cell_of(blocks + j)
            push[ext] += dot_nt(lanes(eight, j).astype(BF16), hot(c_rows[j : j + 1]))
            mine = lanes(eight_n, j)
            n_cell = n_cells[j : j + 1] - ext
            spread = jnp.concatenate([jnp.where(n_cell == offset, mine, 0.0) for offset in offsets], 0)
            out = dot_nt(spread.astype(BF16), hot(n_rows[j : j + 1]))
            for i, offset in enumerate(offsets):
                push[ext + offset] -= out[8 * i : 8 * i + 8]
        return carry

    lax.fori_loop(0, groups, backward, 0)

    for x in range(inner_x + 2):
        for y in range(wide_y):
            both = push[x * wide_y + y]
            total = both[0:4] + both[4:8]
            for m in range(3):
                if x == 0:
                    push_west[m, y : y + 1] = total[m : m + 1]
                elif x == inner_x + 1:
                    push_east[m, y : y + 1] = total[m : m + 1]
                else:
                    push_inner[x - 1, m, y : y + 1] = total[m : m + 1]
            if 1 <= x <= inner_x and 1 <= y <= inner_y:
                energies[x - 1, y - 1 : y] = total[3:4]


def brick(centers, neighbours, live_blocks, table_c, packed, west, east, south, north, *weights):
    inner_x, inner_y, rows, slots = packed.shape
    blocks = centers.shape[2]
    lat = table_c.shape[1]
    ch = weights[2].shape[1]
    wide_y = inner_y + 2
    cells_ext = (inner_x + 2) * wide_y
    groups = blocks // GROUP
    width = GROUP * slots
    vmem = pl.BlockSpec(memory_space=pltpu.VMEM)
    smem = pl.BlockSpec(memory_space=pltpu.SMEM)
    return pl.pallas_call(
        brick_kernel,
        in_specs=[smem, smem] + [vmem] * 14,
        out_specs=(vmem,) * 4,
        out_shape=(
            jax.ShapeDtypeStruct((inner_x, inner_y, slots), F32),
            jax.ShapeDtypeStruct((3, wide_y, slots), F32),
            jax.ShapeDtypeStruct((3, wide_y, slots), F32),
            jax.ShapeDtypeStruct((inner_x, 3, wide_y, slots), F32),
        ),
        scratch_shapes=[
            pltpu.VMEM((cells_ext, rows, slots), F32),
            pltpu.VMEM((inner_x * inner_y, 4 * ch, slots), F32),
            pltpu.VMEM((inner_x * inner_y, 4 * ch, slots), F32),
            pltpu.VMEM((cells_ext, 8, slots), F32),
            pltpu.VMEM((groups, lat, width), F32),
            pltpu.VMEM((groups, lat, width), F32),
            pltpu.VMEM((groups, lat, width), BF16),
            pltpu.VMEM((groups, lat, width), BF16),
            pltpu.VMEM((groups, ch, width), F32),
            pltpu.VMEM((groups, 16, width), F32),
        ],
        compiler_params=pltpu.CompilerParams(vmem_limit_bytes=40 * 1024 * 1024),
    )(centers[0, :, :, 0], live_blocks, centers, neighbours, table_c, packed, west, east, south, north, *weights)


def body(
    features,
    coords,
    centers,
    neighbours,
    live_blocks,
    w_center,
    w_neigh,
    w_radial,
    w_latent,
    w_tensor,
    w_mix,
    w_env,
    w_out,
):
    table_c, packed = tables(features, jnp.swapaxes(coords, 1, 2), w_center, w_neigh)
    inner_x, inner_y = packed.shape[:2]
    west = shifted(packed[inner_x - 1 :], "bx", 1)
    east = shifted(packed[:1], "bx", -1)
    top = jnp.concatenate([west[:, inner_y - 1], packed[:, inner_y - 1], east[:, inner_y - 1]], 0)
    bottom = jnp.concatenate([west[:, 0], packed[:, 0], east[:, 0]], 0)
    south = shifted(top[:, None], "by", 1)
    north = shifted(bottom[:, None], "by", -1)
    weights = (w_radial, w_latent, w_tensor, w_mix, w_env, w_out[:, None])
    energies, push_west, push_east, inner = brick(
        centers, neighbours, live_blocks, table_c, packed, west, east, south, north, *weights
    )
    from_east = shifted(push_west, "bx", -1)
    from_west = shifted(push_east, "bx", 1)
    inner = inner.at[inner_x - 1].add(from_east).at[0].add(from_west)
    from_north = shifted(inner[:, :, 0], "by", -1)
    from_south = shifted(inner[:, :, inner_y + 1], "by", 1)
    forces = inner[:, :, 1 : inner_y + 1]
    forces = forces.at[:, :, inner_y - 1].add(from_north).at[:, :, 0].add(from_south)
    forces = jnp.swapaxes(forces, 1, 2)
    return (energies, forces)


def solution(mesh):
    split_both = P("bx", "by", None, None)
    placed = (split_both,) * 4 + (P("bx", "by"),) + (P(),) * 8
    return jax.shard_map(
        body,
        mesh=mesh,
        in_specs=placed,
        out_specs=(P("bx", "by", None), split_both),
        check_vma=False,
    )
```

```python
import jax
import jax.numpy as jnp
from jax import lax
from jax.experimental import pallas as pl
from jax.experimental.pallas import tpu as pltpu
from jax.sharding import PartitionSpec as P

CELL_WIDTH = 6.0
CUTOFF = 6.0
SOFTEN = 0.25
ROWS = 72
GROUP = 32
F32 = jnp.float32
BF16 = jnp.bfloat16
SMALL = pltpu.CompilerParams(vmem_limit_bytes=8 * 1024 * 1024)
SIN_TERMS = (3.14159265358979, -5.16771278004997, 2.55016403987735, -0.599264529320792, 0.0821458866111282, -0.00737043094571435)
COS_TERMS = (1.0, -4.93480220054468, 4.05871212641677, -1.33526276885459, 0.235330630358893, -0.0258068913900141, 0.00192957430940392)


def swapped(array, axis, far):
    length = lax.axis_size(axis)
    pairs = []
    for low in range(far, length + far, 2):
        pairs += [(low % length, (low + 1) % length), ((low + 1) % length, low % length)]
    return lax.ppermute(array, axis, pairs)


def split(array):
    high = array.astype(BF16).astype(F32)
    return high, array - high


def dot_tn(left, right):
    return lax.dot_general(left, right, (((0,), (0,)), ((), ())), preferred_element_type=F32)


def dot_nt(left, right):
    return lax.dot_general(left, right, (((1,), (1,)), ((), ())), preferred_element_type=F32)


def dot_nn(left, right):
    return jnp.dot(left, right, preferred_element_type=F32)


def tables_kernel(feat, coord, w_both, table_c, packed, send_far, send_near):
    inner_x, inner_y, lat, slots = feat.shape
    both = 0.5 * w_both[...].astype(F32)
    both = jnp.concatenate([both, both], 0).T.astype(BF16)
    pad = jnp.zeros((ROWS - lat - 3, slots), F32)
    for x in range(inner_x):
        flat = jnp.concatenate([feat[x, y] for y in range(inner_y)], 1)
        high, low = split(flat)
        out = dot_nn(both, jnp.concatenate([high, low], 0).astype(BF16))
        for y in range(inner_y):
            piece = out[:, y * slots : (y + 1) * slots]
            table_c[x * inner_y + y] = piece[:lat]
            packed[x, y, :lat] = piece[lat:]
            packed[x, y, lat:] = jnp.concatenate([coord[x, m, y : y + 1] for m in range(3)] + [pad], 0)
    odd = lax.axis_index("bx") % 2
    last = inner_x - 1
    send_far[...] = packed[last * odd]
    send_near[...] = packed[last * (1 - odd)]


def tables(features, coords, w_center, w_neigh):
    inner_x, inner_y, lat, slots = features.shape
    side = jax.ShapeDtypeStruct((inner_y, ROWS, slots), F32)
    return pl.pallas_call(
        tables_kernel,
        out_shape=(
            jax.ShapeDtypeStruct((inner_x * inner_y, lat, slots), F32),
            jax.ShapeDtypeStruct((inner_x, inner_y, ROWS, slots), F32),
            side,
            side,
        ),
        compiler_params=SMALL,
    )(features, coords, jnp.concatenate([w_center, w_neigh], 1))


def sides_kernel(packed, from_far, from_near, send_far, send_near):
    inner_x, inner_y = packed.shape[:2]
    odd_x = lax.axis_index("bx") % 2
    odd_y = lax.axis_index("by") % 2
    for send, odd in ((send_far, odd_y), (send_near, 1 - odd_y)):
        row = (inner_y - 1) * odd
        send[(inner_x + 1) * odd_x] = from_far[row]
        send[(inner_x + 1) * (1 - odd_x)] = from_near[row]
        for x in range(inner_x):
            send[x + 1] = packed[x, row]


def sides(packed, from_far, from_near):
    inner_x, _, rows, slots = packed.shape
    send = jax.ShapeDtypeStruct((inner_x + 2, rows, slots), F32)
    return pl.pallas_call(sides_kernel, out_shape=(send, send), compiler_params=SMALL)(packed, from_far, from_near)


def sine_cosine(turns):
    whole = jnp.floor(turns + 0.5)
    part = turns - whole
    sign = 1.0 - 2.0 * (whole - 2.0 * jnp.floor(0.5 * whole))
    square = part * part

    def poly(terms):
        total = jnp.full_like(square, terms[-1])
        for term in terms[-2::-1]:
            total = total * square + term
        return total

    return sign * part * poly(SIN_TERMS), sign * poly(COS_TERMS)


def gated(half):
    gate = 1.0 + jnp.tanh(half)
    silu = half * gate
    return silu, gate + silu * (2.0 - gate)


def halved(array):
    return (array.astype(F32) * 0.5).astype(array.dtype)


def brick_kernel(
    cells,
    live,
    centers,
    neighbours,
    table_c,
    packed,
    far_x,
    near_x,
    far_y,
    near_y,
    w_radial,
    w_latent,
    w_tensor,
    w_mix,
    w_env,
    w_out,
    energies,
    push_far,
    push_near,
    push_inner,
    table_n,
    gamma,
    g_gamma,
    push,
    slope_z,
    slope_l,
    latent_s,
    g_hidden_s,
    chan_s,
    rows_s,
):
    inner_x, inner_y, _, slots = packed.shape
    wide_y = inner_y + 2
    lat = w_latent.shape[0]
    ch = w_tensor.shape[1]
    nb = w_radial.shape[0]
    width = GROUP * slots
    odd_x = lax.axis_index("bx") % 2
    odd_y = lax.axis_index("by") % 2
    far_x_at = (inner_x + 1) * odd_x
    near_x_at = (inner_x + 1) * (1 - odd_x)
    far_y_at = (inner_y + 1) * odd_y
    near_y_at = (inner_y + 1) * (1 - odd_y)
    for y in range(inner_y):
        for x in range(inner_x):
            table_n[(x + 1) * wide_y + y + 1] = packed[x, y]
        table_n[far_x_at * wide_y + y + 1] = far_x[y]
        table_n[near_x_at * wide_y + y + 1] = near_x[y]
    for x in range(inner_x + 2):
        table_n[x * wide_y + far_y_at] = far_y[x]
        table_n[x * wide_y + near_y_at] = near_y[x]

    gamma[...] = jnp.zeros_like(gamma)
    g_gamma[...] = jnp.zeros_like(g_gamma)
    push[...] = jnp.zeros_like(push)
    wr_high, wr_low = split(0.5 * w_radial[...])
    half_latent, half_mix, half_env = halved(w_latent[...]), halved(w_mix[...]), halved(w_env[...])
    wr_fwd = jnp.concatenate([wr_high, wr_high, wr_low, wr_low], 0).astype(BF16)
    wr_bwd = jnp.concatenate([wr_high, wr_low], 0).astype(BF16)
    orders = lax.broadcasted_iota(jnp.int32, (nb, 1), 0).astype(F32) + 1.0
    slot_iota = lax.broadcasted_iota(jnp.int32, (slots, slots), 0)
    row_iota = lax.broadcasted_iota(jnp.int32, (8, 1), 0)
    force_rows = jnp.where((row_iota & 3) == 3, 0.0, 1.0)
    out_col = w_out[...]
    half_col = 0.5 * out_col
    offsets = [dx * wide_y + dy for dx in (-1, 0, 1) for dy in (-1, 0, 1)]
    groups = (live[0, 0] + (GROUP - 1)) // GROUP
    block_iota = lax.broadcasted_iota(jnp.int32, (1, width), 1) // slots

    def cell_of(block):
        cell = cells[0, block] // slots
        cell_x = cell // inner_y
        return cell, (cell_x + 1) * wide_y + (cell - cell_x * inner_y) + 1

    def hot(slot):
        return jnp.where(slot_iota == slot, 1.0, 0.0).astype(BF16)

    def lanes(array, j):
        return array[:, j * slots : (j + 1) * slots]

    def gathered(table, slot_rows, blocks):
        parts = []
        for j in range(GROUP):
            cell, _ = cell_of(blocks + j)
            index = jnp.broadcast_to(slot_rows[j : j + 1], (4 * ch, slots))
            parts.append(jnp.take_along_axis(table[cell], index, axis=1))
        return jnp.concatenate(parts, 1)

    def scattered(table, values, slot_rows, blocks):
        for j in range(GROUP):
            cell, _ = cell_of(blocks + j)
            out = dot_nt(lanes(values, j).astype(BF16), hot(slot_rows[j : j + 1]))
            rows = table.shape[1]
            table[cell] += sum(out[i : i + rows] for i in range(0, out.shape[0], rows))

    def forward(g, carry):
        blocks = pl.multiple_of(g * GROUP, GROUP)
        c_rows = centers[0, 0, pl.ds(blocks, GROUP), :] & (slots - 1)
        n_all = neighbours[0, 0, pl.ds(blocks, GROUP), :]
        n_rows = n_all & (slots - 1)
        n_cells = n_all >> 7
        n_x = (n_cells * 43) >> 8
        n_y = n_cells - n_x * wide_y
        near_parts, delta_parts = [], []
        for j in range(GROUP):
            cell, ext = cell_of(blocks + j)
            ext_x = cell // inner_y + 1
            ext_y = cell - (ext_x - 1) * inner_y + 1
            c_index = jnp.broadcast_to(c_rows[j : j + 1], (lat, slots))
            n_index = jnp.broadcast_to(n_rows[j : j + 1], (ROWS, slots))
            n_cell = jnp.broadcast_to(n_cells[j : j + 1] - ext, (ROWS, slots))
            near_c = jnp.take_along_axis(table_c[cell], c_index, axis=1)
            place_c = jnp.take_along_axis(table_n[ext, lat:], c_index[:8], axis=1)
            got = jnp.zeros((ROWS, slots), F32)
            for offset in offsets:
                piece = jnp.take_along_axis(table_n[ext + offset], n_index, axis=1)
                got = jnp.where(n_cell == offset, piece, got)
            near_parts.append(near_c + got[:lat])
            step_x = (n_x[j : j + 1] - ext_x).astype(F32) * CELL_WIDTH
            step_y = (n_y[j : j + 1] - ext_y).astype(F32) * CELL_WIDTH
            step = jnp.where(row_iota == 0, step_x, jnp.where(row_iota == 1, step_y, 0.0))
            delta_parts.append(got[lat:] - place_c + step)
        near = jnp.concatenate(near_parts, 1)
        delta = jnp.concatenate(delta_parts, 1)
        square = delta * delta
        length2 = square[0:1] + square[1:2] + square[2:3] + SOFTEN
        inverse = lax.rsqrt(length2)
        scaled = jnp.minimum(length2 * inverse * (1.0 / CUTOFF), 1.0)
        fall = 1.0 - scaled * scaled
        weight = jnp.where(block_iota + blocks < live[0, 0], fall * fall, 0.0)
        harm = delta * inverse
        basis, _ = sine_cosine(orders * scaled)
        b_high, b_low = split(basis)
        b_all = jnp.concatenate([b_high, b_low, b_high, b_low], 0).astype(BF16)
        zeta, slope = gated(near + dot_tn(wr_fwd, b_all))
        slope_z[g] = slope
        latent, slope = gated(dot_tn(half_latent, zeta.astype(BF16)))
        slope_l[g] = slope
        latent = latent.astype(BF16)
        latent_s[g] = latent
        chan = dot_tn(w_tensor[...], latent)
        chan_s[g] = chan
        rows_s[g, 0:3] = harm[0:3]
        rows_s[g, 3:4] = weight
        rows_s[g, 4:5] = scaled
        rows_s[g, 5:6] = inverse
        heavy = chan * weight
        spread = jnp.concatenate([heavy] + [heavy * harm[m : m + 1] for m in range(3)], 0)
        scattered(gamma, jnp.concatenate(split(spread), 0), c_rows, blocks)
        return carry

    lax.fori_loop(0, groups, forward, 0)

    def middle(g, carry):
        blocks = pl.multiple_of(g * GROUP, GROUP)
        c_rows = centers[0, 0, pl.ds(blocks, GROUP), :] & (slots - 1)
        seen = gathered(gamma, c_rows, blocks)
        weight = rows_s[g, 3:4]
        harm = [rows_s[g, m : m + 1] for m in range(3)]
        scal = seen[:ch]
        for m in range(3):
            scal = scal + harm[m] * seen[(m + 1) * ch : (m + 2) * ch]
        hidden = dot_tn(half_mix, latent_s[g]) + dot_tn(half_env, scal.astype(BF16))
        lifted, slope = gated(hidden)
        value = jnp.sum(out_col * lifted, 0, keepdims=True)
        g_hidden = ((half_col * slope) * weight).astype(BF16)
        g_hidden_s[g] = g_hidden
        g_scal = dot_nn(w_env[...], g_hidden)
        rows_s[g, 6:7] = value
        for m in range(3):
            rows_s[g, 8 + m : 9 + m] = jnp.sum(g_scal * seen[(m + 1) * ch : (m + 2) * ch], 0, keepdims=True)
        spread = jnp.concatenate([g_scal] + [g_scal * harm[m] for m in range(3)], 0)
        scattered(g_gamma, spread, c_rows, blocks)
        return carry

    lax.fori_loop(0, groups, middle, 0)

    def backward(g, carry):
        blocks = pl.multiple_of(g * GROUP, GROUP)
        c_rows = centers[0, 0, pl.ds(blocks, GROUP), :] & (slots - 1)
        n_all = neighbours[0, 0, pl.ds(blocks, GROUP), :]
        n_rows = n_all & (slots - 1)
        n_cells = n_all >> 7
        back = gathered(g_gamma, c_rows, blocks)
        harm = [rows_s[g, m : m + 1] for m in range(3)]
        weight = rows_s[g, 3:4]
        scaled = rows_s[g, 4:5]
        inverse = rows_s[g, 5:6]
        value = rows_s[g, 6:7]
        chan = chan_s[g]
        g_weight = value
        g_chan = jnp.zeros_like(chan)
        g_harm = []
        for m in range(4):
            part = back[m * ch : (m + 1) * ch]
            along = jnp.sum(chan * part, 0, keepdims=True)
            if m == 0:
                g_weight = g_weight + along
                g_chan = g_chan + part
            else:
                g_weight = g_weight + along * harm[m - 1]
                g_chan = g_chan + part * harm[m - 1]
                g_harm.append(rows_s[g, 7 + m : 8 + m] + weight * along)
        g_chan = (g_chan * weight).astype(BF16)
        g_latent = dot_nn(w_mix[...], g_hidden_s[g]) + dot_nn(w_tensor[...], g_chan)
        g_zeta = dot_nn(half_latent, (g_latent * slope_l[g]).astype(BF16))
        g_pair = dot_nn(wr_bwd, (g_zeta * slope_z[g]).astype(BF16))
        _, cosines = sine_cosine(orders * scaled)
        turning = (3.14159265358979 * orders) * cosines
        g_scaled = jnp.sum((g_pair[:nb] + g_pair[nb:]) * turning, 0, keepdims=True)
        g_scaled = jnp.where(scaled < 1.0, g_scaled, 0.0)
        g_weight = jnp.where(block_iota + blocks < live[0, 0], g_weight, 0.0)
        g_scaled = g_scaled - 4.0 * scaled * (1.0 - scaled * scaled) * g_weight
        radial = g_harm[0] * harm[0] + g_harm[1] * harm[1] + g_harm[2] * harm[2]
        pull = g_scaled * (1.0 / CUTOFF) - radial * inverse
        grads = [g_harm[m] * inverse + harm[m] * pull for m in range(3)]
        four = jnp.concatenate(grads + [weight * value], 0)
        high, low = split(four)
        eight = jnp.concatenate([high, low], 0)
        eight_n = eight * force_rows
        for j in range(GROUP):
            _, ext = cell_of(blocks + j)
            push[ext] += dot_nt(lanes(eight, j).astype(BF16), hot(c_rows[j : j + 1]))
            mine = lanes(eight_n, j)
            n_cell = n_cells[j : j + 1] - ext
            spread = jnp.concatenate([jnp.where(n_cell == offset, mine, 0.0) for offset in offsets], 0)
            out = dot_nt(spread.astype(BF16), hot(n_rows[j : j + 1]))
            for i, offset in enumerate(offsets):
                push[ext + offset] -= out[8 * i : 8 * i + 8]
        return carry

    lax.fori_loop(0, groups, backward, 0)

    def total(cell):
        both = push[cell]
        return both[0:4] + both[4:8]

    for y in range(wide_y):
        for target, x in ((push_far, far_x_at), (push_near, near_x_at)):
            sums = total(x * wide_y + y)
            for m in range(3):
                target[m, y : y + 1] = sums[m : m + 1]
        for x in range(inner_x):
            sums = total((x + 1) * wide_y + y)
            for m in range(3):
                push_inner[x, m, y : y + 1] = sums[m : m + 1]
            if 1 <= y <= inner_y:
                energies[x, y - 1 : y] = sums[3:4]


def turned_kernel(inner, from_far, from_near, send_far, send_near, kept, work):
    inner_x, _, wide_y, _ = inner.shape
    odd_x = lax.axis_index("bx") % 2
    odd_y = lax.axis_index("by") % 2
    work[...] = inner[...]
    work[(inner_x - 1) * odd_x] += from_far[...]
    work[(inner_x - 1) * (1 - odd_x)] += from_near[...]
    for x in range(inner_x):
        for m in range(3):
            rows = work[x, m]
            low, high = rows[:1], rows[wide_y - 1 :]
            send_far[x, m : m + 1] = jnp.where(odd_y == 1, high, low)
            send_near[x, m : m + 1] = jnp.where(odd_y == 1, low, high)
            kept[x, m] = rows[1 : wide_y - 1]


def turned(inner, from_far, from_near):
    inner_x, _, wide_y, slots = inner.shape
    send = jax.ShapeDtypeStruct((inner_x, 3, slots), F32)
    return pl.pallas_call(
        turned_kernel,
        out_shape=(send, send, jax.ShapeDtypeStruct((inner_x, 3, wide_y - 2, slots), F32)),
        scratch_shapes=[pltpu.VMEM(inner.shape, F32)],
        compiler_params=SMALL,
    )(inner, from_far, from_near)


def final_kernel(kept, from_far, from_near, forces):
    inner_x, _, inner_y, slots = kept.shape
    odd_y = lax.axis_index("by") % 2
    rows = lax.broadcasted_iota(jnp.int32, (inner_y, slots), 0)
    far_at = (inner_y - 1) * odd_y
    near_at = (inner_y - 1) * (1 - odd_y)
    for x in range(inner_x):
        for m in range(3):
            far = jnp.where(rows == far_at, from_far[x, m : m + 1], 0.0)
            near = jnp.where(rows == near_at, from_near[x, m : m + 1], 0.0)
            forces[x, m] = kept[x, m] + far + near


def final(kept, from_far, from_near):
    return pl.pallas_call(
        final_kernel, out_shape=jax.ShapeDtypeStruct(kept.shape, F32), compiler_params=SMALL
    )(kept, from_far, from_near)


def brick(centers, neighbours, live_blocks, table_c, packed, far_x, near_x, far_y, near_y, *weights):
    inner_x, inner_y, rows, slots = packed.shape
    blocks = centers.shape[2]
    lat = table_c.shape[1]
    ch = weights[2].shape[1]
    wide_y = inner_y + 2
    cells_ext = (inner_x + 2) * wide_y
    groups = blocks // GROUP
    width = GROUP * slots
    vmem = pl.BlockSpec(memory_space=pltpu.VMEM)
    smem = pl.BlockSpec(memory_space=pltpu.SMEM)
    return pl.pallas_call(
        brick_kernel,
        in_specs=[smem, smem] + [vmem] * 14,
        out_specs=(vmem,) * 4,
        out_shape=(
            jax.ShapeDtypeStruct((inner_x, inner_y, slots), F32),
            jax.ShapeDtypeStruct((3, wide_y, slots), F32),
            jax.ShapeDtypeStruct((3, wide_y, slots), F32),
            jax.ShapeDtypeStruct((inner_x, 3, wide_y, slots), F32),
        ),
        scratch_shapes=[
            pltpu.VMEM((cells_ext, rows, slots), F32),
            pltpu.VMEM((inner_x * inner_y, 4 * ch, slots), F32),
            pltpu.VMEM((inner_x * inner_y, 4 * ch, slots), F32),
            pltpu.VMEM((cells_ext, 8, slots), F32),
            pltpu.VMEM((groups, lat, width), F32),
            pltpu.VMEM((groups, lat, width), F32),
            pltpu.VMEM((groups, lat, width), BF16),
            pltpu.VMEM((groups, lat, width), BF16),
            pltpu.VMEM((groups, ch, width), F32),
            pltpu.VMEM((groups, 16, width), F32),
        ],
        compiler_params=pltpu.CompilerParams(vmem_limit_bytes=40 * 1024 * 1024),
    )(centers[0, :, :, 0], live_blocks, centers, neighbours, table_c, packed, far_x, near_x, far_y, near_y, *weights)


def body(
    features,
    coords,
    centers,
    neighbours,
    live_blocks,
    w_center,
    w_neigh,
    w_radial,
    w_latent,
    w_tensor,
    w_mix,
    w_env,
    w_out,
):
    table_c, packed, send_far, send_near = tables(features, jnp.swapaxes(coords, 1, 2), w_center, w_neigh)
    inner_x, inner_y = packed.shape[:2]
    far_x = swapped(send_far, "bx", 1)
    near_x = swapped(send_near, "bx", 0)
    send_far, send_near = sides(packed, far_x, near_x)
    far_y = swapped(send_far, "by", 1)
    near_y = swapped(send_near, "by", 0)
    weights = (w_radial, w_latent, w_tensor, w_mix, w_env, w_out[:, None])
    energies, push_far, push_near, inner = brick(
        centers, neighbours, live_blocks, table_c, packed, far_x, near_x, far_y, near_y, *weights
    )
    from_far = swapped(push_far, "bx", 1)
    from_near = swapped(push_near, "bx", 0)
    send_far, send_near, kept = turned(inner, from_far, from_near)
    from_far = swapped(send_far, "by", 1)
    from_near = swapped(send_near, "by", 0)
    forces = jnp.swapaxes(final(kept, from_far, from_near), 1, 2)
    return (energies, forces)


def solution(mesh):
    split_both = P("bx", "by", None, None)
    placed = (split_both,) * 4 + (P("bx", "by"),) + (P(),) * 8
    return jax.shard_map(
        body,
        mesh=mesh,
        in_specs=placed,
        out_specs=(P("bx", "by", None), split_both),
        check_vma=False,
    )
```

```python
import jax
import jax.numpy as jnp
from jax import lax
from jax.experimental import pallas as pl
from jax.experimental.pallas import tpu as pltpu
from jax.sharding import PartitionSpec as P

CELL_WIDTH = 6.0
CUTOFF = 6.0
SOFTEN = 0.25
ROWS = 72
GROUP = 32
HALO_X, HALO_Y, BACK_X, BACK_Y = 0, 0, 0, 0
F32 = jnp.float32
BF16 = jnp.bfloat16
SMALL = pltpu.CompilerParams(vmem_limit_bytes=8 * 1024 * 1024)
SIN_TERMS = (3.14159265358979, -5.16771278004997, 2.55016403987735, -0.599264529320792, 0.0821458866111282, -0.00737043094571435)
COS_TERMS = (1.0, -4.93480220054468, 4.05871212641677, -1.33526276885459, 0.235330630358893, -0.0258068913900141, 0.00192957430940392)


def swapped(array, axis, far):
    length = lax.axis_size(axis)
    pairs = []
    for low in range(far, length + far, 2):
        pairs += [(low % length, (low + 1) % length), ((low + 1) % length, low % length)]
    return lax.ppermute(array, axis, pairs)


def parity(axis, turn):
    return (lax.axis_index(axis) + turn) % 2


def split(array):
    high = array.astype(BF16).astype(F32)
    return high, array - high


def dot_tn(left, right):
    return lax.dot_general(left, right, (((0,), (0,)), ((), ())), preferred_element_type=F32)


def dot_nt(left, right):
    return lax.dot_general(left, right, (((1,), (1,)), ((), ())), preferred_element_type=F32)


def dot_nn(left, right):
    return jnp.dot(left, right, preferred_element_type=F32)


def tables_kernel(feat, coord, w_center, w_neigh, table_c, packed, send_far, send_near):
    inner_x, inner_y, lat, slots = feat.shape
    both = jnp.concatenate([w_center[...].astype(F32), w_neigh[...].astype(F32)], 1)
    both = jnp.concatenate([both, both], 0).T.astype(BF16)
    pad = jnp.zeros((ROWS - lat - 3, slots), F32)
    for x in range(inner_x):
        flat = jnp.concatenate([feat[x, y] for y in range(inner_y)], 1)
        high, low = split(flat)
        out = dot_nn(both, jnp.concatenate([high, low], 0).astype(BF16))
        for y in range(inner_y):
            piece = out[:, y * slots : (y + 1) * slots]
            table_c[x * inner_y + y] = piece[:lat]
            packed[x, y, :lat] = piece[lat:]
            packed[x, y, lat:] = jnp.concatenate([coord[x, m, y : y + 1] for m in range(3)] + [pad], 0)
    odd = parity("bx", HALO_X)
    last = inner_x - 1
    send_far[...] = packed[last * odd]
    send_near[...] = packed[last * (1 - odd)]


def tables(features, coords, w_center, w_neigh):
    inner_x, inner_y, lat, slots = features.shape
    side = jax.ShapeDtypeStruct((inner_y, ROWS, slots), F32)
    return pl.pallas_call(
        tables_kernel,
        out_shape=(
            jax.ShapeDtypeStruct((inner_x * inner_y, lat, slots), F32),
            jax.ShapeDtypeStruct((inner_x, inner_y, ROWS, slots), F32),
            side,
            side,
        ),
        compiler_params=SMALL,
    )(0.5 * features, coords, w_center, w_neigh)


def sides_kernel(
    packed,
    from_far,
    from_near,
    centers,
    neighbours,
    live,
    w_radial,
    w_latent,
    w_tensor,
    w_mix,
    w_env,
    w_out,
    send_far,
    send_near,
    lists,
    wr_all,
    w_latent_o,
    w_tensor_o,
    w_mix_o,
    w_env_o,
    w_out_o,
):
    inner_x, inner_y = packed.shape[:2]
    blocks, slots = centers.shape[2:]
    odd_x = parity("bx", HALO_X)
    odd_y = parity("by", HALO_Y)
    for send, odd in ((send_far, odd_y), (send_near, 1 - odd_y)):
        row = (inner_y - 1) * odd
        send[(inner_x + 1) * odd_x] = from_far[row]
        send[(inner_x + 1) * (1 - odd_x)] = from_near[row]
        for x in range(inner_x):
            send[x + 1] = packed[x, row]
    lists[:blocks] = centers[0, 0]
    lists[blocks : 2 * blocks] = neighbours[0, 0]
    lists[2 * blocks :] = jnp.broadcast_to(live[...], (8, slots))
    high, low = split(0.5 * w_radial[...])
    wr_all[...] = jnp.concatenate([high, high, low, low, high, low], 0).astype(BF16)
    w_latent_o[...] = halved(w_latent[...])
    w_tensor_o[...] = w_tensor[...]
    w_mix_o[...] = w_mix[...]
    w_env_o[...] = w_env[...]
    w_out_o[...] = jnp.broadcast_to(w_out[...], (8, w_out.shape[1])).T[:, :1]


def sides(packed, from_far, from_near, centers, neighbours, live, *weights):
    inner_x, _, rows, slots = packed.shape
    blocks = centers.shape[2]
    nb, lat = weights[0].shape
    send = jax.ShapeDtypeStruct((inner_x + 2, rows, slots), F32)
    same = [jax.ShapeDtypeStruct(w.shape, w.dtype) for w in weights]
    return pl.pallas_call(
        sides_kernel,
        out_shape=(
            send,
            send,
            jax.ShapeDtypeStruct((2 * blocks + 8, slots), jnp.int32),
            jax.ShapeDtypeStruct((6 * nb, lat), BF16),
            *same[1:5],
            jax.ShapeDtypeStruct((lat, 1), F32),
        ),
        compiler_params=SMALL,
    )(packed, from_far, from_near, centers, neighbours, live, *weights)


def sine_cosine(turns):
    whole = jnp.floor(turns + 0.5)
    part = turns - whole
    sign = 1.0 - 2.0 * (whole - 2.0 * jnp.floor(0.5 * whole))
    square = part * part

    def poly(terms):
        total = jnp.full_like(square, terms[-1])
        for term in terms[-2::-1]:
            total = total * square + term
        return total

    return sign * part * poly(SIN_TERMS), sign * poly(COS_TERMS)


def gated(half):
    gate = 1.0 + jnp.tanh(half)
    silu = half * gate
    return silu, gate + silu * (2.0 - gate)


def halved(array):
    return (array.astype(F32) * 0.5).astype(array.dtype)


def brick_kernel(
    lists,
    table_c,
    packed,
    far_x,
    near_x,
    far_y,
    near_y,
    wr_all,
    half_latent,
    w_tensor,
    w_mix,
    w_env,
    w_out,
    energies,
    push_far,
    push_near,
    push_inner,
    table_n,
    gamma,
    g_gamma,
    push,
    slope_z,
    slope_l,
    latent_s,
    g_hidden_s,
    chan_s,
    rows_s,
):
    inner_x, inner_y, _, slots = packed.shape
    wide_y = inner_y + 2
    lat = half_latent.shape[0]
    ch = w_tensor.shape[0]
    nb = wr_all.shape[0] // 6
    count = (lists.shape[0] - 8) // 2
    width = GROUP * slots
    odd_x = parity("bx", HALO_X)
    odd_y = parity("by", HALO_Y)
    far_x_at = (inner_x + 1) * odd_x
    near_x_at = (inner_x + 1) * (1 - odd_x)
    far_y_at = (inner_y + 1) * odd_y
    near_y_at = (inner_y + 1) * (1 - odd_y)
    for y in range(inner_y):
        for x in range(inner_x):
            table_n[(x + 1) * wide_y + y + 1] = packed[x, y]
        table_n[far_x_at * wide_y + y + 1] = far_x[y]
        table_n[near_x_at * wide_y + y + 1] = near_x[y]
    for x in range(inner_x + 2):
        table_n[x * wide_y + far_y_at] = far_y[x]
        table_n[x * wide_y + near_y_at] = near_y[x]

    gamma[...] = jnp.zeros_like(gamma)
    g_gamma[...] = jnp.zeros_like(g_gamma)
    push[...] = jnp.zeros_like(push)
    wr_fwd, wr_bwd = wr_all[: 4 * nb], wr_all[4 * nb :]
    half_mix, half_env = halved(w_mix[...]), halved(w_env[...])
    live = lists[2 * count : 2 * count + 1, :1]
    orders = lax.broadcasted_iota(jnp.int32, (nb, 1), 0).astype(F32) + 1.0
    slot_iota = lax.broadcasted_iota(jnp.int32, (slots, slots), 0)
    row_iota = lax.broadcasted_iota(jnp.int32, (8, 1), 0)
    force_rows = jnp.where((row_iota & 3) == 3, 0.0, 1.0)
    out_col = w_out[...]
    half_col = 0.5 * out_col
    offsets = [dx * wide_y + dy for dx in (-1, 0, 1) for dy in (-1, 0, 1)]
    groups = count // GROUP
    block_iota = lax.broadcasted_iota(jnp.int32, (1, width), 1) // slots

    heads = lists[:count, :1] >> 7
    cells = [heads[block, 0] for block in range(count)]

    def cell_of(block):
        cell = cells[block]
        cell_x = cell // inner_y
        return cell, (cell_x + 1) * wide_y + (cell - cell_x * inner_y) + 1

    def hot(slot):
        return jnp.where(slot_iota == slot, 1.0, 0.0).astype(BF16)

    def lanes(array, j):
        return array[:, j * slots : (j + 1) * slots]

    def gathered(table, slot_rows, blocks):
        parts = []
        for j in range(GROUP):
            cell, _ = cell_of(blocks + j)
            index = jnp.broadcast_to(slot_rows[j : j + 1], (4 * ch, slots))
            parts.append(jnp.take_along_axis(table[cell], index, axis=1))
        return jnp.concatenate(parts, 1)

    def scattered(table, values, slot_rows, blocks):
        for j in range(GROUP):
            cell, _ = cell_of(blocks + j)
            out = dot_nt(lanes(values, j).astype(BF16), hot(slot_rows[j : j + 1]))
            rows = table.shape[1]
            table[cell] += sum(out[i : i + rows] for i in range(0, out.shape[0], rows))

    def forward(g, carry):
        blocks = 0
        c_rows = lists[:GROUP] & (slots - 1)
        n_all = lists[GROUP : 2 * GROUP]
        n_rows = n_all & (slots - 1)
        n_cells = n_all >> 7
        n_x = (n_cells * 43) >> 8
        n_y = n_cells - n_x * wide_y
        near_parts, delta_parts = [], []
        for j in range(GROUP):
            cell, ext = cell_of(blocks + j)
            ext_x = cell // inner_y + 1
            ext_y = cell - (ext_x - 1) * inner_y + 1
            c_index = jnp.broadcast_to(c_rows[j : j + 1], (lat, slots))
            n_index = jnp.broadcast_to(n_rows[j : j + 1], (ROWS, slots))
            n_cell = jnp.broadcast_to(n_cells[j : j + 1] - ext, (ROWS, slots))
            near_c = jnp.take_along_axis(table_c[cell], c_index, axis=1)
            place_c = jnp.take_along_axis(table_n[ext, lat:], c_index[:8], axis=1)
            got = jnp.zeros((ROWS, slots), F32)
            for offset in offsets:
                piece = jnp.take_along_axis(table_n[ext + offset], n_index, axis=1)
                got = jnp.where(n_cell == offset, piece, got)
            near_parts.append(near_c + got[:lat])
            step_x = (n_x[j : j + 1] - ext_x).astype(F32) * CELL_WIDTH
            step_y = (n_y[j : j + 1] - ext_y).astype(F32) * CELL_WIDTH
            step = jnp.where(row_iota == 0, step_x, jnp.where(row_iota == 1, step_y, 0.0))
            delta_parts.append(got[lat:] - place_c + step)
        near = jnp.concatenate(near_parts, 1)
        delta = jnp.concatenate(delta_parts, 1)
        square = delta * delta
        length2 = square[0:1] + square[1:2] + square[2:3] + SOFTEN
        inverse = lax.rsqrt(length2)
        scaled = jnp.minimum(length2 * inverse * (1.0 / CUTOFF), 1.0)
        fall = 1.0 - scaled * scaled
        weight = jnp.where(block_iota + blocks < live, fall * fall, 0.0)
        harm = delta * inverse
        basis, _ = sine_cosine(orders * scaled)
        b_high, b_low = split(basis)
        b_all = jnp.concatenate([b_high, b_low, b_high, b_low], 0).astype(BF16)
        zeta, slope = gated(near + dot_tn(wr_fwd, b_all))
        slope_z[g] = slope
        latent, slope = gated(dot_tn(half_latent[...], zeta.astype(BF16)))
        slope_l[g] = slope
        latent = latent.astype(BF16)
        latent_s[g] = latent
        chan = dot_nn(w_tensor[...], latent)
        chan_s[g] = chan
        rows_s[g, 0:3] = harm[0:3]
        rows_s[g, 3:4] = weight
        rows_s[g, 4:5] = scaled
        rows_s[g, 5:6] = inverse
        heavy = chan * weight
        spread = jnp.concatenate([heavy] + [heavy * harm[m : m + 1] for m in range(3)], 0)
        scattered(gamma, jnp.concatenate(split(spread), 0), c_rows, blocks)
        return carry

    lax.fori_loop(0, groups, forward, 0)

    def middle(g, carry):
        blocks = 0
        c_rows = lists[:GROUP] & (slots - 1)
        seen = gathered(gamma, c_rows, blocks)
        weight = rows_s[g, 3:4]
        harm = [rows_s[g, m : m + 1] for m in range(3)]
        scal = seen[:ch]
        for m in range(3):
            scal = scal + harm[m] * seen[(m + 1) * ch : (m + 2) * ch]
        hidden = dot_tn(half_mix, latent_s[g]) + dot_tn(half_env, scal.astype(BF16))
        lifted, slope = gated(hidden)
        value = jnp.sum(out_col * lifted, 0, keepdims=True)
        g_hidden = ((half_col * slope) * weight).astype(BF16)
        g_hidden_s[g] = g_hidden
        g_scal = dot_nn(w_env[...], g_hidden)
        rows_s[g, 6:7] = value
        for m in range(3):
            rows_s[g, 8 + m : 9 + m] = jnp.sum(g_scal * seen[(m + 1) * ch : (m + 2) * ch], 0, keepdims=True)
        spread = jnp.concatenate([g_scal] + [g_scal * harm[m] for m in range(3)], 0)
        scattered(g_gamma, spread, c_rows, blocks)
        return carry

    lax.fori_loop(0, groups, middle, 0)

    def backward(g, carry):
        blocks = 0
        c_rows = lists[:GROUP] & (slots - 1)
        n_all = lists[GROUP : 2 * GROUP]
        n_rows = n_all & (slots - 1)
        n_cells = n_all >> 7
        back = gathered(g_gamma, c_rows, blocks)
        harm = [rows_s[g, m : m + 1] for m in range(3)]
        weight = rows_s[g, 3:4]
        scaled = rows_s[g, 4:5]
        inverse = rows_s[g, 5:6]
        value = rows_s[g, 6:7]
        chan = chan_s[g]
        g_weight = value
        g_chan = jnp.zeros_like(chan)
        g_harm = []
        for m in range(4):
            part = back[m * ch : (m + 1) * ch]
            along = jnp.sum(chan * part, 0, keepdims=True)
            if m == 0:
                g_weight = g_weight + along
                g_chan = g_chan + part
            else:
                g_weight = g_weight + along * harm[m - 1]
                g_chan = g_chan + part * harm[m - 1]
                g_harm.append(rows_s[g, 7 + m : 8 + m] + weight * along)
        g_chan = (g_chan * weight).astype(BF16)
        g_latent = dot_nn(w_mix[...], g_hidden_s[g]) + dot_tn(w_tensor[...], g_chan)
        g_zeta = dot_nn(half_latent[...], (g_latent * slope_l[g]).astype(BF16))
        g_pair = dot_nn(wr_bwd, (g_zeta * slope_z[g]).astype(BF16))
        _, cosines = sine_cosine(orders * scaled)
        turning = (3.14159265358979 * orders) * cosines
        g_scaled = jnp.sum((g_pair[:nb] + g_pair[nb:]) * turning, 0, keepdims=True)
        g_scaled = jnp.where(scaled < 1.0, g_scaled, 0.0)
        g_weight = jnp.where(block_iota + blocks < live, g_weight, 0.0)
        g_scaled = g_scaled - 4.0 * scaled * (1.0 - scaled * scaled) * g_weight
        radial = g_harm[0] * harm[0] + g_harm[1] * harm[1] + g_harm[2] * harm[2]
        pull = g_scaled * (1.0 / CUTOFF) - radial * inverse
        grads = [g_harm[m] * inverse + harm[m] * pull for m in range(3)]
        four = jnp.concatenate(grads + [weight * value], 0)
        high, low = split(four)
        eight = jnp.concatenate([high, low], 0)
        eight_n = eight * force_rows
        for j in range(GROUP):
            _, ext = cell_of(blocks + j)
            push[ext] += dot_nt(lanes(eight, j).astype(BF16), hot(c_rows[j : j + 1]))
            mine = lanes(eight_n, j)
            n_cell = n_cells[j : j + 1] - ext
            spread = jnp.concatenate([jnp.where(n_cell == offset, mine, 0.0) for offset in offsets], 0)
            out = dot_nt(spread.astype(BF16), hot(n_rows[j : j + 1]))
            for i, offset in enumerate(offsets):
                push[ext + offset] -= out[8 * i : 8 * i + 8]
        return carry

    lax.fori_loop(0, groups, backward, 0)

    def total(cell):
        both = push[cell]
        return both[0:4] + both[4:8]

    odd_x = parity("bx", BACK_X)
    far_at, near_at = (inner_x + 1) * odd_x, (inner_x + 1) * (1 - odd_x)
    for y in range(wide_y):
        for target, x in ((push_far, far_at), (push_near, near_at)):
            sums = total(x * wide_y + y)
            for m in range(3):
                target[m, y : y + 1] = sums[m : m + 1]
        for x in range(inner_x):
            sums = total((x + 1) * wide_y + y)
            for m in range(3):
                push_inner[x, m, y : y + 1] = sums[m : m + 1]
            if 1 <= y <= inner_y:
                energies[x, y - 1 : y] = sums[3:4]


def turned_kernel(inner, from_far, from_near, send_near, send_far, kept, work):
    inner_x, _, wide_y, _ = inner.shape
    odd_x = parity("bx", BACK_X)
    odd_y = parity("by", BACK_Y)
    work[...] = inner[...]
    work[(inner_x - 1) * odd_x] += from_far[...]
    work[(inner_x - 1) * (1 - odd_x)] += from_near[...]
    for x in range(inner_x):
        for m in range(3):
            rows = work[x, m]
            low, high = rows[:1], rows[wide_y - 1 :]
            send_far[x, m : m + 1] = jnp.where(odd_y == 1, high, low)
            send_near[x, m : m + 1] = jnp.where(odd_y == 1, low, high)
            kept[x, m] = rows[1 : wide_y - 1]


def turned(inner, from_far, from_near):
    inner_x, _, wide_y, slots = inner.shape
    send = jax.ShapeDtypeStruct((inner_x, 3, slots), F32)
    return pl.pallas_call(
        turned_kernel,
        out_shape=(send, send, jax.ShapeDtypeStruct((inner_x, 3, wide_y - 2, slots), F32)),
        scratch_shapes=[pltpu.VMEM(inner.shape, F32)],
        compiler_params=SMALL,
    )(inner, from_far, from_near)


def final_kernel(kept, from_near, from_far, forces):
    inner_x, _, inner_y, slots = kept.shape
    odd_y = parity("by", BACK_Y)
    rows = lax.broadcasted_iota(jnp.int32, (inner_y, slots), 0)
    far_at = (inner_y - 1) * odd_y
    near_at = (inner_y - 1) * (1 - odd_y)
    for x in range(inner_x):
        for m in range(3):
            far = jnp.where(rows == far_at, from_far[x, m : m + 1], 0.0)
            near = jnp.where(rows == near_at, from_near[x, m : m + 1], 0.0)
            forces[x, m] = kept[x, m] + far + near


def final(kept, from_near, from_far):
    return pl.pallas_call(
        final_kernel, out_shape=jax.ShapeDtypeStruct(kept.shape, F32), compiler_params=SMALL
    )(kept, from_near, from_far)


def brick(lists, table_c, packed, far_x, near_x, far_y, near_y, *weights):
    inner_x, inner_y, rows, slots = packed.shape
    blocks = (lists.shape[0] - 8) // 2
    lat = table_c.shape[1]
    ch = weights[2].shape[0]
    wide_y = inner_y + 2
    cells_ext = (inner_x + 2) * wide_y
    groups = blocks // GROUP
    width = GROUP * slots
    return pl.pallas_call(
        brick_kernel,
        out_shape=(
            jax.ShapeDtypeStruct((inner_x, inner_y, slots), F32),
            jax.ShapeDtypeStruct((3, wide_y, slots), F32),
            jax.ShapeDtypeStruct((3, wide_y, slots), F32),
            jax.ShapeDtypeStruct((inner_x, 3, wide_y, slots), F32),
        ),
        scratch_shapes=[
            pltpu.VMEM((cells_ext, rows, slots), F32),
            pltpu.VMEM((inner_x * inner_y, 4 * ch, slots), F32),
            pltpu.VMEM((inner_x * inner_y, 4 * ch, slots), F32),
            pltpu.VMEM((cells_ext, 8, slots), F32),
            pltpu.VMEM((groups, lat, width), F32),
            pltpu.VMEM((groups, lat, width), F32),
            pltpu.VMEM((groups, lat, width), BF16),
            pltpu.VMEM((groups, lat, width), BF16),
            pltpu.VMEM((groups, ch, width), F32),
            pltpu.VMEM((groups, 16, width), F32),
        ],
        compiler_params=pltpu.CompilerParams(vmem_limit_bytes=40 * 1024 * 1024),
    )(lists, table_c, packed, far_x, near_x, far_y, near_y, *weights)


def body(
    features,
    coords,
    centers,
    neighbours,
    live_blocks,
    w_center,
    w_neigh,
    w_radial,
    w_latent,
    w_tensor,
    w_mix,
    w_env,
    w_out,
):
    table_c, packed, send_far, send_near = tables(features, jnp.swapaxes(coords, 1, 2), w_center, w_neigh)
    inner_x, inner_y = packed.shape[:2]
    far_x = swapped(send_far, "bx", 1 - HALO_X)
    near_x = swapped(send_near, "bx", HALO_X)
    weights = (w_radial, w_latent, w_tensor.T, w_mix, w_env, w_out[None])
    send_far, send_near, *operands = sides(packed, far_x, near_x, centers, neighbours, live_blocks, *weights)
    far_y = swapped(send_far, "by", 1 - HALO_Y)
    near_y = swapped(send_near, "by", HALO_Y)
    lists, *weights = operands
    energies, push_far, push_near, inner = brick(lists, table_c, packed, far_x, near_x, far_y, near_y, *weights)
    from_far = swapped(push_far, "bx", 1 - BACK_X)
    from_near = swapped(push_near, "bx", BACK_X)
    send_near, send_far, kept = turned(inner, from_far, from_near)
    from_near = swapped(send_near, "by", BACK_Y)
    from_far = swapped(send_far, "by", 1 - BACK_Y)
    forces = jnp.swapaxes(final(kept, from_near, from_far), 1, 2)
    return (energies, forces)


def solution(mesh):
    split_both = P("bx", "by", None, None)
    placed = (split_both,) * 4 + (P("bx", "by"),) + (P(),) * 8
    return jax.shard_map(
        body,
        mesh=mesh,
        in_specs=placed,
        out_specs=(P("bx", "by", None), split_both),
        check_vma=False,
    )
```

```python
import jax
import jax.numpy as jnp
from jax import lax
from jax.experimental import pallas as pl
from jax.experimental.pallas import tpu as pltpu
from jax.sharding import PartitionSpec as P

CELL_WIDTH = 6.0
CUTOFF = 6.0
SOFTEN = 0.25
ROWS = 72
GROUP = 32
HALO_X, HALO_Y, BACK_X, BACK_Y = 0, 0, 0, 0
F32 = jnp.float32
BF16 = jnp.bfloat16
SMALL = pltpu.CompilerParams(vmem_limit_bytes=8 * 1024 * 1024)
SIN_TERMS = (3.14159265358979, -5.16771278004997, 2.55016403987735, -0.599264529320792, 0.0821458866111282, -0.00737043094571435)
COS_TERMS = (1.0, -4.93480220054468, 4.05871212641677, -1.33526276885459, 0.235330630358893, -0.0258068913900141, 0.00192957430940392)


def swapped(array, axis, far):
    length = lax.axis_size(axis)
    pairs = []
    for low in range(far, length + far, 2):
        pairs += [(low % length, (low + 1) % length), ((low + 1) % length, low % length)]
    return lax.ppermute(array, axis, pairs)


def parity(axis, turn):
    return (lax.axis_index(axis) + turn) % 2


def split(array):
    high = array.astype(BF16).astype(F32)
    return high, array - high


def dot_tn(left, right):
    return lax.dot_general(left, right, (((0,), (0,)), ((), ())), preferred_element_type=F32)


def dot_nt(left, right):
    return lax.dot_general(left, right, (((1,), (1,)), ((), ())), preferred_element_type=F32)


def dot_nn(left, right):
    return jnp.dot(left, right, preferred_element_type=F32)


def tables_kernel(feat, coord, w_center, w_neigh, table_c, packed, send_far, send_near):
    inner_x, inner_y, lat, slots = feat.shape
    both = jnp.concatenate([w_center[...].astype(F32), w_neigh[...].astype(F32)], 1)
    both = jnp.concatenate([both, both], 0).T.astype(BF16)
    pad = jnp.zeros((ROWS - lat - 3, slots), F32)
    for x in range(inner_x):
        flat = jnp.concatenate([feat[x, y] for y in range(inner_y)], 1)
        high, low = split(flat)
        out = dot_nn(both, jnp.concatenate([high, low], 0).astype(BF16))
        for y in range(inner_y):
            piece = out[:, y * slots : (y + 1) * slots]
            table_c[x * inner_y + y] = piece[:lat]
            packed[x, y, :lat] = piece[lat:]
            packed[x, y, lat:] = jnp.concatenate([coord[x, m, y : y + 1] for m in range(3)] + [pad], 0)
    odd = parity("bx", HALO_X)
    last = inner_x - 1
    send_far[...] = packed[last * odd]
    send_near[...] = packed[last * (1 - odd)]


def tables(features, coords, w_center, w_neigh):
    inner_x, inner_y, lat, slots = features.shape
    side = jax.ShapeDtypeStruct((inner_y, ROWS, slots), F32)
    return pl.pallas_call(
        tables_kernel,
        out_shape=(
            jax.ShapeDtypeStruct((inner_x * inner_y, lat, slots), F32),
            jax.ShapeDtypeStruct((inner_x, inner_y, ROWS, slots), F32),
            side,
            side,
        ),
        compiler_params=SMALL,
    )(0.5 * features, coords, w_center, w_neigh)


def sides_kernel(
    packed,
    from_far,
    from_near,
    centers,
    neighbours,
    live,
    w_radial,
    w_latent,
    w_tensor,
    w_mix,
    w_env,
    send_far,
    send_near,
    lists,
    wr_all,
    w_latent_o,
    w_tensor_o,
    w_mix_o,
    w_env_o,
    w_out_o,
):
    inner_x, inner_y = packed.shape[:2]
    blocks, slots = centers.shape[2:]
    odd_x = parity("bx", HALO_X)
    odd_y = parity("by", HALO_Y)
    for send, odd in ((send_far, odd_y), (send_near, 1 - odd_y)):
        row = (inner_y - 1) * odd
        send[(inner_x + 1) * odd_x] = from_far[row]
        send[(inner_x + 1) * (1 - odd_x)] = from_near[row]
        for x in range(inner_x):
            send[x + 1] = packed[x, row]
    lists[:blocks] = centers[0, 0]
    lists[blocks : 2 * blocks] = neighbours[0, 0]
    lists[2 * blocks :] = jnp.broadcast_to(live[...], (8, slots))
    nb = w_radial.shape[0] - 1
    high, low = split(0.5 * w_radial[:nb])
    wr_all[...] = jnp.concatenate([high, high, low, low, high, low], 0).astype(BF16)
    w_latent_o[...] = halved(w_latent[...])
    w_tensor_o[...] = w_tensor[...]
    w_mix_o[...] = w_mix[...]
    w_env_o[...] = w_env[...]
    w_out_o[...] = jnp.broadcast_to(w_radial[nb:], (8, w_radial.shape[1])).T[:, :1]


def sides(packed, from_far, from_near, centers, neighbours, live, *weights):
    inner_x, _, rows, slots = packed.shape
    blocks = centers.shape[2]
    nb, lat = weights[0].shape[0] - 1, weights[0].shape[1]
    send = jax.ShapeDtypeStruct((inner_x + 2, rows, slots), F32)
    same = [jax.ShapeDtypeStruct(w.shape, w.dtype) for w in weights]
    return pl.pallas_call(
        sides_kernel,
        out_shape=(
            send,
            send,
            jax.ShapeDtypeStruct((2 * blocks + 8, slots), jnp.int32),
            jax.ShapeDtypeStruct((6 * nb, lat), BF16),
            *same[1:],
            jax.ShapeDtypeStruct((lat, 1), F32),
        ),
        compiler_params=SMALL,
    )(packed, from_far, from_near, centers, neighbours, live, *weights)


def sine_cosine(turns):
    whole = jnp.floor(turns + 0.5)
    part = turns - whole
    sign = 1.0 - 2.0 * (whole - 2.0 * jnp.floor(0.5 * whole))
    square = part * part

    def poly(terms):
        total = jnp.full_like(square, terms[-1])
        for term in terms[-2::-1]:
            total = total * square + term
        return total

    return sign * part * poly(SIN_TERMS), sign * poly(COS_TERMS)


def gated(half):
    gate = 1.0 + jnp.tanh(half)
    silu = half * gate
    return silu, gate + silu * (2.0 - gate)


def halved(array):
    return (array.astype(F32) * 0.5).astype(array.dtype)


def brick_kernel(
    lists,
    table_c,
    packed,
    far_x,
    near_x,
    far_y,
    near_y,
    wr_all,
    half_latent,
    w_tensor,
    w_mix,
    w_env,
    w_out,
    energies,
    push_far,
    push_near,
    push_inner,
    table_n,
    gamma,
    g_gamma,
    push,
    slope_z,
    slope_l,
    latent_s,
    g_hidden_s,
    chan_s,
    rows_s,
):
    inner_x, inner_y, _, slots = packed.shape
    wide_y = inner_y + 2
    lat = half_latent.shape[0]
    ch = w_tensor.shape[0]
    nb = wr_all.shape[0] // 6
    count = (lists.shape[0] - 8) // 2
    width = GROUP * slots
    odd_x = parity("bx", HALO_X)
    odd_y = parity("by", HALO_Y)
    far_x_at = (inner_x + 1) * odd_x
    near_x_at = (inner_x + 1) * (1 - odd_x)
    far_y_at = (inner_y + 1) * odd_y
    near_y_at = (inner_y + 1) * (1 - odd_y)
    for y in range(inner_y):
        for x in range(inner_x):
            table_n[(x + 1) * wide_y + y + 1] = packed[x, y]
        table_n[far_x_at * wide_y + y + 1] = far_x[y]
        table_n[near_x_at * wide_y + y + 1] = near_x[y]
    for x in range(inner_x + 2):
        table_n[x * wide_y + far_y_at] = far_y[x]
        table_n[x * wide_y + near_y_at] = near_y[x]

    gamma[...] = jnp.zeros_like(gamma)
    g_gamma[...] = jnp.zeros_like(g_gamma)
    push[...] = jnp.zeros_like(push)
    wr_fwd, wr_bwd = wr_all[: 4 * nb], wr_all[4 * nb :]
    half_mix, half_env = halved(w_mix[...]), halved(w_env[...])
    live = lists[2 * count : 2 * count + 1, :1]
    orders = lax.broadcasted_iota(jnp.int32, (nb, 1), 0).astype(F32) + 1.0
    slot_iota = lax.broadcasted_iota(jnp.int32, (slots, slots), 0)
    row_iota = lax.broadcasted_iota(jnp.int32, (8, 1), 0)
    force_rows = jnp.where((row_iota & 3) == 3, 0.0, 1.0)
    out_col = w_out[...]
    half_col = 0.5 * out_col
    offsets = [dx * wide_y + dy for dx in (-1, 0, 1) for dy in (-1, 0, 1)]
    groups = count // GROUP
    block_iota = lax.broadcasted_iota(jnp.int32, (1, width), 1) // slots

    heads = lists[:count, :1] >> 7
    cells = [heads[block, 0] for block in range(count)]

    def cell_of(block):
        cell = cells[block]
        cell_x = cell // inner_y
        return cell, (cell_x + 1) * wide_y + (cell - cell_x * inner_y) + 1

    def hot(slot):
        return jnp.where(slot_iota == slot, 1.0, 0.0).astype(BF16)

    def lanes(array, j):
        return array[:, j * slots : (j + 1) * slots]

    def gathered(table, slot_rows, blocks):
        parts = []
        for j in range(GROUP):
            cell, _ = cell_of(blocks + j)
            index = jnp.broadcast_to(slot_rows[j : j + 1], (4 * ch, slots))
            parts.append(jnp.take_along_axis(table[cell], index, axis=1))
        return jnp.concatenate(parts, 1)

    def scattered(table, values, slot_rows, blocks):
        for j in range(GROUP):
            cell, _ = cell_of(blocks + j)
            out = dot_nt(lanes(values, j).astype(BF16), hot(slot_rows[j : j + 1]))
            rows = table.shape[1]
            table[cell] += sum(out[i : i + rows] for i in range(0, out.shape[0], rows))

    def forward(g, carry):
        blocks = 0
        c_rows = lists[:GROUP] & (slots - 1)
        n_all = lists[GROUP : 2 * GROUP]
        n_rows = n_all & (slots - 1)
        n_cells = n_all >> 7
        n_x = (n_cells * 43) >> 8
        n_y = n_cells - n_x * wide_y
        near_parts, delta_parts = [], []
        for j in range(GROUP):
            cell, ext = cell_of(blocks + j)
            ext_x = cell // inner_y + 1
            ext_y = cell - (ext_x - 1) * inner_y + 1
            c_index = jnp.broadcast_to(c_rows[j : j + 1], (lat, slots))
            n_index = jnp.broadcast_to(n_rows[j : j + 1], (ROWS, slots))
            n_cell = jnp.broadcast_to(n_cells[j : j + 1] - ext, (ROWS, slots))
            near_c = jnp.take_along_axis(table_c[cell], c_index, axis=1)
            place_c = jnp.take_along_axis(table_n[ext, lat:], c_index[:8], axis=1)
            got = jnp.zeros((ROWS, slots), F32)
            for offset in offsets:
                piece = jnp.take_along_axis(table_n[ext + offset], n_index, axis=1)
                got = jnp.where(n_cell == offset, piece, got)
            near_parts.append(near_c + got[:lat])
            step_x = (n_x[j : j + 1] - ext_x).astype(F32) * CELL_WIDTH
            step_y = (n_y[j : j + 1] - ext_y).astype(F32) * CELL_WIDTH
            step = jnp.where(row_iota == 0, step_x, jnp.where(row_iota == 1, step_y, 0.0))
            delta_parts.append(got[lat:] - place_c + step)
        near = jnp.concatenate(near_parts, 1)
        delta = jnp.concatenate(delta_parts, 1)
        square = delta * delta
        length2 = square[0:1] + square[1:2] + square[2:3] + SOFTEN
        inverse = lax.rsqrt(length2)
        scaled = jnp.minimum(length2 * inverse * (1.0 / CUTOFF), 1.0)
        fall = 1.0 - scaled * scaled
        weight = jnp.where(block_iota + blocks < live, fall * fall, 0.0)
        harm = delta * inverse
        basis, _ = sine_cosine(orders * scaled)
        b_high, b_low = split(basis)
        b_all = jnp.concatenate([b_high, b_low, b_high, b_low], 0).astype(BF16)
        zeta, slope = gated(near + dot_tn(wr_fwd, b_all))
        slope_z[g] = slope
        latent, slope = gated(dot_tn(half_latent[...], zeta.astype(BF16)))
        slope_l[g] = slope
        latent = latent.astype(BF16)
        latent_s[g] = latent
        chan = dot_nn(w_tensor[...], latent)
        chan_s[g] = chan
        rows_s[g, 0:3] = harm[0:3]
        rows_s[g, 3:4] = weight
        rows_s[g, 4:5] = scaled
        rows_s[g, 5:6] = inverse
        heavy = chan * weight
        spread = jnp.concatenate([heavy] + [heavy * harm[m : m + 1] for m in range(3)], 0)
        scattered(gamma, jnp.concatenate(split(spread), 0), c_rows, blocks)
        return carry

    lax.fori_loop(0, groups, forward, 0)

    def middle(g, carry):
        blocks = 0
        c_rows = lists[:GROUP] & (slots - 1)
        seen = gathered(gamma, c_rows, blocks)
        weight = rows_s[g, 3:4]
        harm = [rows_s[g, m : m + 1] for m in range(3)]
        scal = seen[:ch]
        for m in range(3):
            scal = scal + harm[m] * seen[(m + 1) * ch : (m + 2) * ch]
        hidden = dot_tn(half_mix, latent_s[g]) + dot_tn(half_env, scal.astype(BF16))
        lifted, slope = gated(hidden)
        value = jnp.sum(out_col * lifted, 0, keepdims=True)
        g_hidden = ((half_col * slope) * weight).astype(BF16)
        g_hidden_s[g] = g_hidden
        g_scal = dot_nn(w_env[...], g_hidden)
        rows_s[g, 6:7] = value
        for m in range(3):
            rows_s[g, 8 + m : 9 + m] = jnp.sum(g_scal * seen[(m + 1) * ch : (m + 2) * ch], 0, keepdims=True)
        spread = jnp.concatenate([g_scal] + [g_scal * harm[m] for m in range(3)], 0)
        scattered(g_gamma, spread, c_rows, blocks)
        return carry

    lax.fori_loop(0, groups, middle, 0)

    def backward(g, carry):
        blocks = 0
        c_rows = lists[:GROUP] & (slots - 1)
        n_all = lists[GROUP : 2 * GROUP]
        n_rows = n_all & (slots - 1)
        n_cells = n_all >> 7
        back = gathered(g_gamma, c_rows, blocks)
        harm = [rows_s[g, m : m + 1] for m in range(3)]
        weight = rows_s[g, 3:4]
        scaled = rows_s[g, 4:5]
        inverse = rows_s[g, 5:6]
        value = rows_s[g, 6:7]
        chan = chan_s[g]
        g_weight = value
        g_chan = jnp.zeros_like(chan)
        g_harm = []
        for m in range(4):
            part = back[m * ch : (m + 1) * ch]
            along = jnp.sum(chan * part, 0, keepdims=True)
            if m == 0:
                g_weight = g_weight + along
                g_chan = g_chan + part
            else:
                g_weight = g_weight + along * harm[m - 1]
                g_chan = g_chan + part * harm[m - 1]
                g_harm.append(rows_s[g, 7 + m : 8 + m] + weight * along)
        g_chan = (g_chan * weight).astype(BF16)
        g_latent = dot_nn(w_mix[...], g_hidden_s[g]) + dot_tn(w_tensor[...], g_chan)
        g_zeta = dot_nn(half_latent[...], (g_latent * slope_l[g]).astype(BF16))
        g_pair = dot_nn(wr_bwd, (g_zeta * slope_z[g]).astype(BF16))
        _, cosines = sine_cosine(orders * scaled)
        turning = (3.14159265358979 * orders) * cosines
        g_scaled = jnp.sum((g_pair[:nb] + g_pair[nb:]) * turning, 0, keepdims=True)
        g_scaled = jnp.where(scaled < 1.0, g_scaled, 0.0)
        g_weight = jnp.where(block_iota + blocks < live, g_weight, 0.0)
        g_scaled = g_scaled - 4.0 * scaled * (1.0 - scaled * scaled) * g_weight
        radial = g_harm[0] * harm[0] + g_harm[1] * harm[1] + g_harm[2] * harm[2]
        pull = g_scaled * (1.0 / CUTOFF) - radial * inverse
        grads = [g_harm[m] * inverse + harm[m] * pull for m in range(3)]
        four = jnp.concatenate(grads + [weight * value], 0)
        high, low = split(four)
        eight = jnp.concatenate([high, low], 0)
        eight_n = eight * force_rows
        for j in range(GROUP):
            _, ext = cell_of(blocks + j)
            push[ext] += dot_nt(lanes(eight, j).astype(BF16), hot(c_rows[j : j + 1]))
            mine = lanes(eight_n, j)
            n_cell = n_cells[j : j + 1] - ext
            spread = jnp.concatenate([jnp.where(n_cell == offset, mine, 0.0) for offset in offsets], 0)
            out = dot_nt(spread.astype(BF16), hot(n_rows[j : j + 1]))
            for i, offset in enumerate(offsets):
                push[ext + offset] -= out[8 * i : 8 * i + 8]
        return carry

    lax.fori_loop(0, groups, backward, 0)

    def total(cell):
        both = push[cell]
        return both[0:4] + both[4:8]

    odd_x = parity("bx", BACK_X)
    far_at, near_at = (inner_x + 1) * odd_x, (inner_x + 1) * (1 - odd_x)
    for y in range(wide_y):
        for target, x in ((push_far, far_at), (push_near, near_at)):
            sums = total(x * wide_y + y)
            for m in range(3):
                target[m, y : y + 1] = sums[m : m + 1]
        for x in range(inner_x):
            sums = total((x + 1) * wide_y + y)
            for m in range(3):
                push_inner[x, m, y : y + 1] = sums[m : m + 1]
            if 1 <= y <= inner_y:
                energies[x, y - 1 : y] = sums[3:4]


def turned_kernel(inner, from_far, from_near, send_near, send_far, kept, work):
    inner_x, _, wide_y, _ = inner.shape
    odd_x = parity("bx", BACK_X)
    odd_y = parity("by", BACK_Y)
    work[...] = inner[...]
    work[(inner_x - 1) * odd_x] += from_far[...]
    work[(inner_x - 1) * (1 - odd_x)] += from_near[...]
    for x in range(inner_x):
        for m in range(3):
            rows = work[x, m]
            low, high = rows[:1], rows[wide_y - 1 :]
            send_far[x, m : m + 1] = jnp.where(odd_y == 1, high, low)
            send_near[x, m : m + 1] = jnp.where(odd_y == 1, low, high)
            kept[x, m] = rows[1 : wide_y - 1]


def turned(inner, from_far, from_near):
    inner_x, _, wide_y, slots = inner.shape
    send = jax.ShapeDtypeStruct((inner_x, 3, slots), F32)
    return pl.pallas_call(
        turned_kernel,
        out_shape=(send, send, jax.ShapeDtypeStruct((inner_x, 3, wide_y - 2, slots), F32)),
        scratch_shapes=[pltpu.VMEM(inner.shape, F32)],
        compiler_params=SMALL,
    )(inner, from_far, from_near)


def final_kernel(kept, from_near, from_far, forces):
    inner_x, _, inner_y, slots = kept.shape
    odd_y = parity("by", BACK_Y)
    rows = lax.broadcasted_iota(jnp.int32, (inner_y, slots), 0)
    far_at = (inner_y - 1) * odd_y
    near_at = (inner_y - 1) * (1 - odd_y)
    for x in range(inner_x):
        for m in range(3):
            far = jnp.where(rows == far_at, from_far[x, m : m + 1], 0.0)
            near = jnp.where(rows == near_at, from_near[x, m : m + 1], 0.0)
            forces[x, m] = kept[x, m] + far + near


def final(kept, from_near, from_far):
    return pl.pallas_call(
        final_kernel, out_shape=jax.ShapeDtypeStruct(kept.shape, F32), compiler_params=SMALL
    )(kept, from_near, from_far)


def brick(lists, table_c, packed, far_x, near_x, far_y, near_y, *weights):
    inner_x, inner_y, rows, slots = packed.shape
    blocks = (lists.shape[0] - 8) // 2
    lat = table_c.shape[1]
    ch = weights[2].shape[0]
    wide_y = inner_y + 2
    cells_ext = (inner_x + 2) * wide_y
    groups = blocks // GROUP
    width = GROUP * slots
    return pl.pallas_call(
        brick_kernel,
        out_shape=(
            jax.ShapeDtypeStruct((inner_x, inner_y, slots), F32),
            jax.ShapeDtypeStruct((3, wide_y, slots), F32),
            jax.ShapeDtypeStruct((3, wide_y, slots), F32),
            jax.ShapeDtypeStruct((inner_x, 3, wide_y, slots), F32),
        ),
        scratch_shapes=[
            pltpu.VMEM((cells_ext, rows, slots), F32),
            pltpu.VMEM((inner_x * inner_y, 4 * ch, slots), F32),
            pltpu.VMEM((inner_x * inner_y, 4 * ch, slots), F32),
            pltpu.VMEM((cells_ext, 8, slots), F32),
            pltpu.VMEM((groups, lat, width), F32),
            pltpu.VMEM((groups, lat, width), F32),
            pltpu.VMEM((groups, lat, width), BF16),
            pltpu.VMEM((groups, lat, width), BF16),
            pltpu.VMEM((groups, ch, width), F32),
            pltpu.VMEM((groups, 16, width), F32),
        ],
        compiler_params=pltpu.CompilerParams(vmem_limit_bytes=40 * 1024 * 1024),
    )(lists, table_c, packed, far_x, near_x, far_y, near_y, *weights)


def body(
    features,
    coords,
    centers,
    neighbours,
    live_blocks,
    w_center,
    w_neigh,
    w_radial,
    w_latent,
    w_tensor,
    w_mix,
    w_env,
    w_out,
):
    table_c, packed, send_far, send_near = tables(features, jnp.swapaxes(coords, 1, 2), w_center, w_neigh)
    inner_x, inner_y = packed.shape[:2]
    far_x = swapped(send_far, "bx", 1 - HALO_X)
    near_x = swapped(send_near, "bx", HALO_X)
    weights = (jnp.concatenate([w_radial, w_out[None]], 0), w_latent, w_tensor.T, w_mix, w_env)
    send_far, send_near, *operands = sides(packed, far_x, near_x, centers, neighbours, live_blocks, *weights)
    far_y = swapped(send_far, "by", 1 - HALO_Y)
    near_y = swapped(send_near, "by", HALO_Y)
    lists, *weights = operands
    energies, push_far, push_near, inner = brick(lists, table_c, packed, far_x, near_x, far_y, near_y, *weights)
    from_far = swapped(push_far, "bx", 1 - BACK_X)
    from_near = swapped(push_near, "bx", BACK_X)
    send_near, send_far, kept = turned(inner, from_far, from_near)
    from_near = swapped(send_near, "by", BACK_Y)
    from_far = swapped(send_far, "by", 1 - BACK_Y)
    forces = jnp.swapaxes(final(kept, from_near, from_far), 1, 2)
    return (energies, forces)


def solution(mesh):
    split_both = P("bx", "by", None, None)
    placed = (split_both,) * 4 + (P("bx", "by"),) + (P(),) * 8
    return jax.shard_map(
        body,
        mesh=mesh,
        in_specs=placed,
        out_specs=(P("bx", "by", None), split_both),
        check_vma=False,
    )
```
